512 devices in a mesh: event: 4 (over x), tile: 128 (over z, y, core).
Axes of the slice: x: 4, y: 4, z: 16, core: 2. Of those that a mesh axis runs over, the one named last changes fastest.
Arguments:
- fine: bfloat16 [4, 10240, 32, 256], P('event', 'tile'), may hold values from -6 to 6
- cotangent: bfloat16 [4, 10240, 32, 256], P('event', 'tile'), may hold values from -6 to 6
- counts: int32 [4, 128], P('event', 'tile'), may hold values from 40 to 80, as said below
- parent: int32 [4, 10240], P('event', 'tile'), may hold values from 0 to 2559, as said below
- quadrant: int32 [4, 10240], P('event', 'tile'), may hold values from 0 to 3
- down_weight: bfloat16 [4, 32, 128], replicated, may hold values from -0.5 to 0.5
- mid_weight: bfloat16 [9, 128, 128], replicated, may hold values from -0.1875 to 0.1875
- up_weight: bfloat16 [4, 32, 128], replicated, may hold values from -0.5 to 0.5
Outputs:
- grad_fine: bfloat16 [4, 10240, 32, 256], P('event', 'tile')
- grad_down: float32 [4, 32, 128], replicated
- grad_mid: float32 [9, 128, 128], replicated
- grad_up: float32 [4, 32, 128], replicated
The draws below stay inside these ranges and needn't reach their ends.
Inputs may be any that keep to these rules, and one draw needn't show every extreme that they name: `counts`: one device of each readout has 80. Among the active tiles of a readout no two share both parent and quadrant. Coarse tile p is owned by device p // 20 along tile. At most 1 active tiles of one device have parents owned by one device, and in every readout some device reaches 1 for some owner.
All inputs are finite; a program needn't handle non-finite values.
Results may differ from the reference program's by a relative error of at most 0.0068.
Values may be sent and summed in bfloat16 or wider, within the bound.
A program may use at most 128 MiB of HBM per device.

```python
import math
import jax
import jax.numpy as jnp
from jax import lax

FINE_CH = 32
COARSE_CH = 128
FINE_DEV = 80
COARSE_DEV = 20
CAP = 1
EVENTS = 4
FINE = 10240
COARSE = 2560
N_TILE = 128


def tile_routes(base_key):

    def one_event(event_key):
        pick_key, row_key, cell_key = jax.random.split(event_key, 3)
        spread = FINE_DEV // CAP
        offset_ids = jnp.arange(N_TILE, dtype=jnp.int32)
        ranks = jax.random.permutation(pick_key, N_TILE).astype(jnp.int32)
        ranks = jnp.where(offset_ids == 1, -3, jnp.where(offset_ids == N_TILE - 1, -2, jnp.where(offset_ids == N_TILE // 2, -1, ranks)))
        offsets = jnp.argsort(ranks, stable=True)[:spread].astype(jnp.int32)
        row_perms = jax.vmap(lambda sub_key: jax.random.permutation(sub_key, FINE_DEV))(jax.random.split(row_key, N_TILE)).astype(jnp.int32)
        cell_perms = jax.vmap(lambda sub_key: jax.random.permutation(sub_key, FINE_DEV))(jax.random.split(cell_key, N_TILE)).astype(jnp.int32)
        group_index = row_perms // CAP
        within = row_perms % CAP
        device = jnp.arange(N_TILE, dtype=jnp.int32)[:, None]
        owners = (device + offsets[group_index]) % N_TILE
        local_slot = group_index * CAP + within
        child_cell = cell_perms[owners, local_slot]
        parents = owners * COARSE_DEV + child_cell // 4
        quarters = child_cell % 4
        return (parents.reshape(-1), quarters.reshape(-1))
    return jax.vmap(one_event)(jax.random.split(base_key, EVENTS))


def draw_parent(key, part):
    parents, quarters = tile_routes(jax.random.fold_in(key, 7))
    return parents.astype(jnp.int32)


def draw_quadrant(key, part):
    parents, quarters = tile_routes(jax.random.fold_in(key, 7))
    return quarters.astype(jnp.int32)


def draw_counts(key, part):
    spread_key, full_key = jax.random.split(jax.random.fold_in(key, 11))
    half_rows = FINE_DEV // 2
    rest_rows = FINE_DEV - half_rows
    uniform_int = jax.random.randint(spread_key, (EVENTS, N_TILE), 0, 65)
    loads = half_rows + rest_rows * uniform_int * uniform_int // 4096
    fullest = jax.random.randint(full_key, (EVENTS, 1), 0, N_TILE)
    columns = jnp.arange(N_TILE, dtype=jnp.int32)[None, :]
    return jnp.where(columns == fullest, FINE_DEV, loads).astype(jnp.int32)


def shard_levels(rng, dims, shards, smallest, high):
    factor_of = 1.0
    for position, shards_of in shards:
        steps = jax.random.uniform(jax.random.fold_in(jax.random.fold_in(rng, 6), position), (shards_of,), jnp.float32, smallest / len(shards), high / len(shards))
        factor_of = factor_of * jnp.repeat(jnp.exp(steps), dims[position] // shards_of).reshape((-1,) + (1,) * (len(dims) - 1 - position))
    return factor_of


def bell_draw(own_key, shape, width, reach, cuts=(), kind=jnp.bfloat16):
    entries = jax.random.normal(own_key, shape, jnp.float32) * width
    if len(cuts) > 0:
        entries = shard_levels(own_key, shape, cuts, -0.22, 0.18) * entries
    return jnp.clip(entries, min=-reach, max=reach).astype(kind)


def setup_inputs(seed: int = 0) -> dict:
    key_of = jax.random.split(jax.random.key(seed), 9)
    fine = bell_draw(key_of[0], (EVENTS, FINE, FINE_CH, 256), 1.0, 6.0, ((0, 4), (1, 128)))
    cotangent = bell_draw(key_of[1], (EVENTS, FINE, FINE_CH, 256), 1.0, 6.0, ((0, 4), (1, 128)))
    counts = draw_counts(jax.random.fold_in(key_of[8], 71), 0)
    parent = draw_parent(jax.random.fold_in(key_of[8], 71), 0)
    quadrant = draw_quadrant(jax.random.fold_in(key_of[8], 71), 0)
    down_weight = bell_draw(key_of[5], (4, FINE_CH, COARSE_CH), (4 * FINE_CH) ** -0.5, 0.5)
    mid_weight = bell_draw(key_of[6], (9, COARSE_CH, COARSE_CH), (9 * COARSE_CH) ** -0.5, 0.1875)
    up_weight = bell_draw(key_of[7], (4, FINE_CH, COARSE_CH), COARSE_CH ** -0.5, 0.5)
    return {"fine": fine, "cotangent": cotangent, "counts": counts, "parent": parent, "quadrant": quadrant, "down_weight": down_weight, "mid_weight": mid_weight, "up_weight": up_weight}


def silu_slope(inputs):
    logistic = jax.nn.sigmoid(inputs)
    return logistic * (1.0 + inputs * (1.0 - logistic))

def split_taps(tile_rows):
    number, channels = (tile_rows.shape[0], tile_rows.shape[1])
    blocks = tile_rows.reshape(number, channels, 8, 2, 8, 2)
    return blocks.transpose(0, 2, 4, 3, 5, 1).reshape(number, 64, 4 * channels)

def join_taps(tap_rows, channels):
    number = tap_rows.shape[0]
    blocks = tap_rows.reshape(number, 8, 8, 2, 2, channels)
    return blocks.transpose(0, 5, 1, 3, 2, 4).reshape(number, channels, 256)

def quads_to_grid(quarters):
    number = quarters.shape[0] // 4
    channels = quarters.shape[2]
    blocks = quarters.reshape(number, 2, 2, 8, 8, channels)
    return blocks.transpose(0, 1, 3, 2, 4, 5).reshape(number, 256, channels)

def grid_to_quads(coarse_grid):
    number, channels = (coarse_grid.shape[0], coarse_grid.shape[2])
    blocks = coarse_grid.reshape(number, 2, 8, 2, 8, channels)
    return blocks.transpose(0, 1, 3, 2, 4, 5).reshape(number * 4, 64, channels)

def shifted(coarse_grid, row_off, col_off):
    number, channels = (coarse_grid.shape[0], coarse_grid.shape[2])
    padded = jnp.pad(coarse_grid.reshape(number, 16, 16, channels), ((0, 0), (1, 1), (1, 1), (0, 0)))
    return padded[:, row_off:row_off + 16, col_off:col_off + 16, :].reshape(number, 256, channels)

def patches(coarse_grid, flip):
    pieces = []
    for row_off in range(3):
        for col_off in range(3):
            if flip:
                pieces.append(shifted(coarse_grid, 2 - row_off, 2 - col_off))
            else:
                pieces.append(shifted(coarse_grid, row_off, col_off))
    return jnp.concatenate(pieces, axis=2).reshape(-1, 9 * coarse_grid.shape[2])

def owner_terms(child_x, child_g, down_weight, mid_weight, up_weight):
    fine_ch = child_x.shape[1]
    coarse_ch = down_weight.shape[2]
    down_flat = down_weight.reshape(4 * fine_ch, coarse_ch)
    up_flat = up_weight.reshape(4 * fine_ch, coarse_ch)
    mid_flat = mid_weight.reshape(9 * coarse_ch, coarse_ch)
    mid_back = jnp.transpose(mid_weight, (0, 2, 1)).reshape(9 * coarse_ch, coarse_ch)
    x_taps = split_taps(child_x).reshape(-1, 4 * fine_ch)
    pre_act = jnp.dot(x_taps, down_flat, preferred_element_type=jnp.float32)
    act_quads = jax.nn.silu(pre_act).astype(jnp.bfloat16).reshape(-1, 64, coarse_ch)
    act_grid = quads_to_grid(act_quads)
    act_patch = patches(act_grid, False)
    mid_pre = jnp.dot(act_patch, mid_flat, preferred_element_type=jnp.float32)
    out_grid = (act_grid.reshape(-1, coarse_ch) + jax.nn.silu(mid_pre)).astype(jnp.bfloat16)
    out_quads = grid_to_quads(out_grid.reshape(-1, 256, coarse_ch)).reshape(-1, coarse_ch)
    g_taps = split_taps(child_g).reshape(-1, 4 * fine_ch)
    grad_out_q = jnp.dot(g_taps, up_flat, preferred_element_type=jnp.float32).astype(jnp.bfloat16)
    grad_up = jnp.dot(g_taps.T, out_quads, preferred_element_type=jnp.float32)
    grad_out_grid = quads_to_grid(grad_out_q.reshape(-1, 64, coarse_ch)).reshape(-1, coarse_ch)
    grad_mid_pre = (grad_out_grid * silu_slope(mid_pre)).astype(jnp.bfloat16)
    grad_mid = jnp.dot(act_patch.T, grad_mid_pre, preferred_element_type=jnp.float32)
    back_patch = patches(grad_mid_pre.reshape(-1, 256, coarse_ch), True)
    grad_act = (grad_out_grid + jnp.dot(back_patch, mid_back, preferred_element_type=jnp.float32)).astype(jnp.bfloat16)
    grad_act_q = grid_to_quads(grad_act.reshape(-1, 256, coarse_ch)).reshape(-1, coarse_ch)
    grad_pre = (grad_act_q * silu_slope(pre_act)).astype(jnp.bfloat16)
    grad_down = jnp.dot(x_taps.T, grad_pre, preferred_element_type=jnp.float32)
    fine_back = jnp.dot(grad_pre, down_flat.T, preferred_element_type=jnp.float32)
    grad_child = (child_g + join_taps(fine_back.reshape(-1, 64, 4 * fine_ch), fine_ch)).astype(jnp.bfloat16)
    return (grad_child, grad_down, grad_mid, grad_up)

def reference(fine, cotangent, counts, parent, quadrant, down_weight, mid_weight, up_weight):
    grad_scale = 1.0 / math.sqrt(EVENTS * FINE * 64)

    def event_terms(operands):
        tile_rows, cot_rows, count_row, parent_row, quad_row = operands
        positions = jnp.arange(FINE, dtype=jnp.int32)
        active = positions % FINE_DEV < jnp.take(count_row, positions // FINE_DEV)
        cell_index = jnp.where(active, parent_row * 4 + quad_row, COARSE * 4).astype(jnp.int32)
        child_x = jnp.zeros((COARSE * 4, FINE_CH, 256), jnp.bfloat16).at[cell_index].set(tile_rows, mode='drop')
        child_g = jnp.zeros((COARSE * 4, FINE_CH, 256), jnp.bfloat16).at[cell_index].set(cot_rows, mode='drop')
        blocks_x = child_x.reshape(N_TILE, COARSE_DEV * 4, FINE_CH, 256)
        blocks_g = child_g.reshape(N_TILE, COARSE_DEV * 4, FINE_CH, 256)

        def one_owner(pair):
            return owner_terms(pair[0], pair[1], down_weight, mid_weight, up_weight)
        grad_child, grad_down, grad_mid, grad_up = lax.map(one_owner, (blocks_x, blocks_g))
        grad_child = grad_child.reshape(COARSE * 4, FINE_CH, 256)
        picked = jnp.take(grad_child, jnp.clip(cell_index, 0, COARSE * 4 - 1).astype(jnp.int32), axis=0)
        grad_tiles = jnp.where(active[:, None, None], picked, jnp.zeros((), picked.dtype))
        return (grad_tiles, lax.optimization_barrier(jnp.sum(grad_down, axis=0)), lax.optimization_barrier(jnp.sum(grad_mid, axis=0)), lax.optimization_barrier(jnp.sum(grad_up, axis=0)))
    grad_fine, grad_down, grad_mid, grad_up = lax.map(event_terms, (fine, cotangent, counts, parent, quadrant))
    grad_down = (lax.optimization_barrier(jnp.sum(grad_down, axis=0)) * grad_scale).reshape(4, FINE_CH, COARSE_CH)
    grad_mid = (lax.optimization_barrier(jnp.sum(grad_mid, axis=0)) * grad_scale).reshape(9, COARSE_CH, COARSE_CH)
    grad_up = (lax.optimization_barrier(jnp.sum(grad_up, axis=0)) * grad_scale).reshape(4, FINE_CH, COARSE_CH)
    return (grad_fine, grad_down, grad_mid, grad_up)
```

```python
import functools
import math

import jax
import jax.numpy as jnp
from jax import lax
from jax.experimental import pallas as pl
from jax.experimental.pallas import tpu as pltpu
from jax.sharding import PartitionSpec as P

MESH = pl.DeviceIdType.MESH
F32 = jnp.float32
BF16 = jnp.bfloat16
CHUNK = 8
PIXELS = 64
UP_ROWS = 48
DOWN_ROWS = 32
VMEM_LIMIT = 48 * 1024 * 1024


def mm(a, b):
    return jnp.dot(a, b, preferred_element_type=F32)


def mm_nt(a, b):
    return lax.dot_general(a, b, (((1,), (1,)), ((), ())), preferred_element_type=F32)


def mm_tn(a, b):
    return lax.dot_general(a, b, (((0,), (0,)), ((), ())), preferred_element_type=F32)


def sigmoid(v):
    return 1.0 / (1.0 + jnp.exp(-v))


def slope(v):
    g = sigmoid(v)
    return g * (1.0 + v * (1.0 - g))


def shift8(x, step, fill=None):
    if step == 0:
        return x
    place = lax.broadcasted_iota(jnp.int32, x.shape, 1)
    moved = pltpu.roll(x, 7 if step > 0 else 1, 1)
    outside = place == (7 if step > 0 else 0)
    if fill is None:
        return jnp.where(outside, 0.0, moved)
    return jnp.where(outside, pltpu.roll(fill, 7 if step > 0 else 1, 1), moved)


def write_patches(x, patch_ref, flip):
    number = x.shape[0] // PIXELS
    blocks = x.reshape(number * 8, 8, 128)
    for sx in range(3):
        col_step = 1 - sx if flip else sx - 1
        moved = shift8(blocks, col_step).reshape(number, 8, 8, 128)
        for sy in range(3):
            row_step = 1 - sy if flip else sy - 1
            zero = jnp.zeros((number, 1, 8, 128), F32)
            if row_step > 0:
                value = jnp.concatenate([moved[:, 1:], zero], axis=1)
            elif row_step < 0:
                value = jnp.concatenate([zero, moved[:, :7]], axis=1)
            else:
                value = moved
            tap = 3 * sy + sx
            patch_ref[:, tap * 128 : (tap + 1) * 128] = value.reshape(number * PIXELS, 128).astype(BF16)


def spread_weight(weight_ref, spread_ref):
    spread_ref[...] = jnp.zeros_like(spread_ref)
    for tap in range(4):
        for tile in range(4):
            row = tap * 128 + tile * 32
            spread_ref[row : row + 32, tile * 128 : (tile + 1) * 128] = weight_ref[tap]


def to_lanes(x):
    groups = x.shape[0] // (4 * PIXELS)
    rows = []
    for group in range(groups):
        parts = [
            x[(group * 4 + tile) * PIXELS : (group * 4 + tile + 1) * PIXELS] for tile in range(4)
        ]
        rows.append(jnp.concatenate(parts, axis=1))
    return jnp.concatenate(rows, axis=0)


def to_rows(x):
    groups = x.shape[0] // PIXELS
    parts = []
    for group in range(groups):
        for tile in range(4):
            parts.append(x[group * PIXELS : (group + 1) * PIXELS, tile * 128 : (tile + 1) * 128])
    return jnp.concatenate(parts, axis=0)


def taps_of(select, tiles):
    return mm_nt(select, tiles)


def taps_to_lanes(x):
    groups = x.shape[1] // 128
    rows = []
    for group in range(groups):
        parts = [
            x[tap * PIXELS : (tap + 1) * PIXELS, group * 128 : (group + 1) * 128]
            for tap in range(4)
        ]
        rows.append(jnp.concatenate(parts, axis=1))
    return jnp.concatenate(rows, axis=0)


def lanes_to_taps(x):
    groups = x.shape[0] // PIXELS
    columns = []
    for group in range(groups):
        parts = [
            x[group * PIXELS : (group + 1) * PIXELS, tap * 128 : (tap + 1) * 128]
            for tap in range(4)
        ]
        columns.append(jnp.concatenate(parts, axis=0))
    return jnp.concatenate(columns, axis=1)


def holder_first(
    coarse_dev,
    count_ref,
    parent_ref,
    quad_ref,
    fine_ref,
    cot_ref,
    select_ref,
    down_ref,
    up_ref,
    mid_ref,
    x_ref,
    g_ref,
    pre_ref,
    local_ref,
    grad_out_ref,
    send_ref,
    down_s,
    up_s,
    patch_s,
    act_s,
    out_s,
):
    step = pl.program_id(0)
    base = step * CHUNK
    count = count_ref[0]

    @pl.when(step == 0)
    def _():
        spread_weight(down_ref, down_s)
        spread_weight(up_ref, up_s)
        send_ref[...] = jnp.full(send_ref.shape, -1.0, BF16)

    select = select_ref[...]
    x_taps = taps_to_lanes(taps_of(select, fine_ref[...].reshape(CHUNK * 32, 256)).astype(BF16))
    x_ref[...] = x_taps
    pre = to_rows(mm(x_taps, down_s[...]))
    pre_ref[...] = pre
    act = (pre * sigmoid(pre)).astype(BF16).astype(F32)
    act_s[...] = act
    write_patches(act, patch_s, False)

    g_taps = taps_of(select, cot_ref[...].reshape(CHUNK * 32, 256))
    tile_of = lax.broadcasted_iota(jnp.int32, g_taps.shape, 1) // 32
    g_taps = taps_to_lanes(jnp.where(tile_of + base < count, g_taps, 0.0).astype(BF16))
    g_ref[...] = g_taps
    grad_out = to_rows(mm(g_taps, up_s[...])).astype(BF16)
    grad_out_ref[...] = grad_out
    out_s[...] = grad_out.astype(F32)

    local_ref[...] = mm(patch_s[...], mid_ref[...])

    for tile in range(CHUNK):
        parent = parent_ref[base + tile]
        quad = quad_ref[base + tile]
        owner = parent // coarse_dev
        cell = (parent - owner * coarse_dev) * 4 + quad
        low = quad // 2
        edge_y = (1 - low) * 7
        edge_x = (1 - quad % 2) * 7
        parts = []
        for source in (act_s, local_ref, out_s):
            row = source[pl.ds(pl.multiple_of(tile * PIXELS + 8 * edge_y, 8), 8), :]
            col = source[pl.ds(tile * PIXELS + edge_x, 8, stride=8), :]
            col = jnp.where(low == 1, pltpu.roll(col, 7, 0), col)
            parts += [row, col]
        place = lax.broadcasted_iota(jnp.int32, (8, 128), 0)
        parts[5] = jnp.where(place == 7, cell.astype(F32), parts[5])

        @pl.when(base + tile < count)
        def _():
            send_ref[owner] = jnp.concatenate(parts, axis=0).astype(BF16)


def owner_edges(tag_ref, got_ref, mid_ref, back_ref, send_ref, cross_ref, edge_s, reply_s):
    slots = got_ref.shape[0]
    rows = edge_s.shape[2] - 8
    number = rows // 8
    edge_s[...] = jnp.zeros_like(edge_s)

    def take(slot, carry):
        tag = tag_ref[slot]
        cell = jnp.where(tag < 0, number * 4, tag)
        tile, quad = cell // 4, cell % 4
        block = got_ref[slot].astype(F32)
        for kind in range(6):
            part = block[kind * 8 : (kind + 1) * 8]
            if kind % 2 == 1:
                part = jnp.where(quad >= 2, pltpu.roll(part, 1, 0), part)
            edge_s[kind, quad, pl.ds(pl.multiple_of(tile * 8, 8), 8), :] = part
        return carry

    lax.fori_loop(0, slots, take, 0, unroll=4)

    def edge(kind, quad):
        return edge_s[kind, quad, :rows, :].reshape(number, 8, 128)

    place = lax.broadcasted_iota(jnp.int32, (number, 8, 128), 1)

    def corner(x, at):
        return jnp.broadcast_to(x[:, at : at + 1, :], x.shape)

    def side(parts):
        return jnp.concatenate(
            [part.reshape(rows, 128).astype(BF16) for part in parts], axis=1
        )

    grad_row, grad_col = [], []
    for quad in range(4):
        low, right = quad // 2, quad % 2
        at_y, at_x = 7 - 7 * low, 7 - 7 * right
        across, beyond = edge(0, quad ^ 2), edge(0, quad ^ 3)
        beside = edge(1, quad ^ 1)
        fills = [beyond if right == 1 else None, None, beyond if right == 0 else None]
        sy, sx = 2 - 2 * low, 2 - 2 * right
        patch = side([shift8(across, s - 1, fills[s]) for s in range(3)])
        weight = mid_ref[3 * sy * 128 : (3 * sy + 3) * 128]
        row = mm(patch, weight).reshape(number, 8, 128)
        patch = side([shift8(beside, s - 1) for s in range(3)])
        weight = jnp.concatenate(
            [mid_ref[(3 * s + sx) * 128 : (3 * s + sx + 1) * 128] for s in range(3)], axis=0
        )
        col = mm(patch, weight).reshape(number, 8, 128)
        row_sum = row + jnp.where(place == at_x, corner(col, at_y), 0.0)
        col_sum = col + jnp.where(place == at_y, corner(row, at_x), 0.0)
        reply_s[0, quad, :rows, :] = row_sum.reshape(rows, 128)
        reply_s[1, quad, :rows, :] = jnp.where(place == at_y, 0.0, col).reshape(rows, 128)
        go_row = edge(4, quad)
        go_col = jnp.where(place == at_y, corner(go_row, at_x), edge(5, quad))
        grad_row.append((go_row * slope(edge(2, quad) + row_sum)).astype(BF16).astype(F32))
        grad_col.append((go_col * slope(edge(3, quad) + col_sum)).astype(BF16).astype(F32))

    cross_ref[...] = jnp.zeros_like(cross_ref)
    for quad in range(4):
        low, right = quad // 2, quad % 2
        at_y, at_x = 7 - 7 * low, 7 - 7 * right
        across, beyond, beside = grad_row[quad ^ 2], grad_row[quad ^ 3], grad_col[quad ^ 1]
        sy, sx = 2 * low, 2 * right
        fills = [beyond if right == 0 else None, None, beyond if right == 1 else None]
        patch = side([shift8(across, 1 - s, fills[s]) for s in range(3)])
        row = mm(patch, back_ref[3 * sy * 128 : (3 * sy + 3) * 128]).reshape(number, 8, 128)
        act_row = edge_s[0, quad, :rows, :].astype(BF16)
        cross_ref[:, 3 * sy * 128 : (3 * sy + 3) * 128] += mm_tn(act_row, patch)
        patch = side([shift8(beside, 1 - s) for s in range(3)])
        weight = jnp.concatenate(
            [back_ref[(3 * s + sx) * 128 : (3 * s + sx + 1) * 128] for s in range(3)], axis=0
        )
        col = mm(patch, weight).reshape(number, 8, 128)
        act_col = edge_s[1, quad, :rows, :].astype(BF16)
        part = mm_tn(act_col, patch)
        for s in range(3):
            tap = 3 * s + sx
            cross_ref[:, tap * 128 : (tap + 1) * 128] += part[:, s * 128 : (s + 1) * 128]
        row_sum = row + jnp.where(place == at_x, corner(col, at_y), 0.0)
        reply_s[2, quad, :rows, :] = row_sum.reshape(rows, 128)
        reply_s[3, quad, :rows, :] = jnp.where(place == at_y, 0.0, col).reshape(rows, 128)

    reply_s[:, :, rows:, :] = jnp.zeros((4, 4, 8, 128), F32)

    def give(slot, carry):
        tag = tag_ref[slot]
        cell = jnp.where(tag < 0, number * 4, tag)
        tile, quad = cell // 4, cell % 4
        parts = [
            reply_s[kind, quad, pl.ds(pl.multiple_of(tile * 8, 8), 8), :] for kind in range(4)
        ]
        send_ref[slot] = jnp.concatenate(parts, axis=0).astype(BF16)
        return carry

    lax.fori_loop(0, slots, give, 0, unroll=4)


def holder_last(
    coarse_dev,
    scale,
    count_ref,
    parent_ref,
    quad_ref,
    cot_ref,
    x_ref,
    g_ref,
    pre_ref,
    local_ref,
    grad_out_ref,
    got_ref,
    cross_ref,
    select_ref,
    down_ref,
    back_ref,
    fine_ref,
    weights_ref,
    down_s,
    patch_s,
    mid_s,
    act_s,
    mid_acc,
    down_acc,
    up_acc,
):
    step = pl.program_id(0)
    base = step * CHUNK
    count = count_ref[0]

    @pl.when(step == 0)
    def _():
        spread_weight(down_ref, down_s)
        mid_acc[...] = cross_ref[...]
        down_acc[...] = jnp.zeros_like(down_acc)
        up_acc[...] = jnp.zeros_like(up_acc)

    def add_edges(target, first):
        for tile in range(CHUNK):

            @pl.when(base + tile < count)
            def _():
                owner = parent_ref[base + tile] // coarse_dev
                quad = quad_ref[base + tile]
                edge_y = (1 - quad // 2) * 7
                edge_x = (1 - quad % 2) * 7
                block = got_ref[owner, first : first + 16, :].astype(F32)
                at_row = pl.ds(pl.multiple_of(tile * PIXELS + 8 * edge_y, 8), 8)
                target[at_row, :] += block[:8]
                at_col = pl.ds(tile * PIXELS + edge_x, 8, stride=8)
                target[at_col, :] += block[8:]

    mid_s[...] = local_ref[...]
    add_edges(mid_s, 0)
    mid = mid_s[...]
    gate = sigmoid(mid)
    pre = pre_ref[...]
    pre_gate = sigmoid(pre)
    act = (pre * pre_gate).astype(BF16)
    out = (act.astype(F32) + mid * gate).astype(BF16)
    grad_out = grad_out_ref[...].astype(F32)
    grad_mid_pre = (grad_out * (gate * (1.0 + mid * (1.0 - gate)))).astype(BF16)
    write_patches(grad_mid_pre.astype(F32), patch_s, True)
    act_s[...] = grad_out + mm(patch_s[...], back_ref[...])
    add_edges(act_s, 16)
    mid_acc[...] += mm_tn(act, patch_s[...])
    up_acc[...] += mm_tn(g_ref[...], to_lanes(out))
    grad_act = act_s[...].astype(BF16).astype(F32)
    grad_pre = (grad_act * (pre_gate * (1.0 + pre * (1.0 - pre_gate)))).astype(BF16)
    grad_pre = to_lanes(grad_pre)
    down_acc[...] += mm_tn(x_ref[...], grad_pre)
    back = lanes_to_taps(mm_nt(grad_pre, down_s[...]))
    high = back.astype(BF16)
    rest = (back - high.astype(F32)).astype(BF16)
    select = select_ref[...]
    fine_back = mm_tn(high, select) + mm_tn(rest, select)
    total = cot_ref[...].reshape(CHUNK * 32, 256).astype(F32) + fine_back
    tile_of = lax.broadcasted_iota(jnp.int32, total.shape, 0) // 32
    total = jnp.where(tile_of + base < count, total, 0.0)
    fine_ref[...] = total.astype(BF16).reshape(CHUNK, 32, 256)

    @pl.when(step == pl.num_programs(0) - 1)
    def _():
        for tap in range(9):
            weights_ref[tap * 128 : (tap + 1) * 128, :] = (
                mid_acc[:, tap * 128 : (tap + 1) * 128] * scale
            ).astype(BF16)
        for index, acc in enumerate((down_acc, up_acc)):
            for tap in range(4):
                part = jnp.zeros((32, 128), F32)
                for tile in range(4):
                    row = tap * 128 + tile * 32
                    part += acc[row : row + 32, tile * 128 : (tile + 1) * 128]
                row = 1152 + index * 128 + tap * 32
                weights_ref[row : row + 32, :] = (part * scale).astype(BF16)
        weights_ref[1408:, :] = jnp.zeros((weights_ref.shape[0] - 1408, 128), BF16)


def sum_weights(
    events, plane, depth, pieces, mine_ref, total_ref, near_s, sum_s, far_s, fin_s, low_s, all_s,
    near_send, near_recv, far_send, far_recv, fin_send, fin_recv, all_send, all_recv,
):
    event = lax.axis_index("event")
    tile = lax.axis_index("tile")
    z = tile // plane
    low = tile % plane
    group = events * plane
    me = event * plane + low
    share = mine_ref.shape[0] // group
    piece = share // pieces

    def near_id(p):
        return (p // plane, z * plane + p % plane)

    def far_id(p):
        return (event, p * plane + low)

    barrier = pltpu.get_barrier_semaphore()

    def greet_near(k, carry):
        pl.semaphore_signal(
            barrier, inc=1, device_id=near_id((me + k) % group), device_id_type=MESH
        )
        return carry

    def greet_far(k, carry):
        pl.semaphore_signal(
            barrier, inc=1, device_id=far_id((z + k) % depth), device_id_type=MESH
        )
        return carry

    lax.fori_loop(1, group, greet_near, 0)
    lax.fori_loop(1, depth, greet_far, 0)
    pl.semaphore_wait(barrier, group + depth - 2)

    def rows(p):
        return pl.ds(pl.multiple_of(p * share, 16), share)

    def near_copy(to, slot):
        return pltpu.make_async_remote_copy(
            src_ref=mine_ref.at[rows(to)],
            dst_ref=near_s.at[slot],
            send_sem=near_send.at[to],
            recv_sem=near_recv.at[slot],
            device_id=near_id(to),
            device_id_type=MESH,
        )

    def send_near(k, carry):
        near_copy((me + k) % group, me).start()
        return carry

    lax.fori_loop(1, group, send_near, 0)

    def take_near(k, total):
        p = (me + k) % group
        near_copy(p, p).wait_recv()
        return total + near_s[p].astype(F32)

    total = lax.fori_loop(1, group, take_near, mine_ref[rows(me), :].astype(F32))
    sum_s[...] = total.reshape(pieces, piece, 128)

    def far_copy(to, slot):
        return pltpu.make_async_remote_copy(
            src_ref=sum_s.at[to],
            dst_ref=far_s.at[slot],
            send_sem=far_send.at[to],
            recv_sem=far_recv.at[slot],
            device_id=far_id(to),
            device_id_type=MESH,
        )

    for to in range(pieces):

        @pl.when(z != to)
        def _():
            far_copy(to, z).start()

    def fin_copy(to, slot):
        return pltpu.make_async_remote_copy(
            src_ref=fin_s.at[slot],
            dst_ref=fin_s.at[slot],
            send_sem=fin_send.at[to],
            recv_sem=fin_recv.at[slot],
            device_id=far_id(to),
            device_id_type=MESH,
        )

    @pl.when(z < pieces)
    def _():
        def take_far(k, total):
            p = (z + k) % depth
            far_copy(z, p).wait_recv()
            return total + far_s[p]

        fin_s[z] = lax.fori_loop(1, depth, take_far, sum_s[z])

        def send_fin(k, carry):
            fin_copy((z + k) % depth, z).start()
            return carry

        lax.fori_loop(1, depth, send_fin, 0)

    for p in range(pieces):

        @pl.when(z != p)
        def _():
            fin_copy(p, p).wait_recv()

    low_s[...] = fin_s[...].reshape(share, 128).astype(BF16)

    def all_copy(to, slot):
        return pltpu.make_async_remote_copy(
            src_ref=low_s,
            dst_ref=all_s.at[rows(slot)],
            send_sem=all_send.at[to],
            recv_sem=all_recv.at[slot],
            device_id=near_id(to),
            device_id_type=MESH,
        )

    def send_all(k, carry):
        all_copy((me + k) % group, me).start()
        return carry

    lax.fori_loop(1, group, send_all, 0)
    all_s[rows(me), :] = low_s[...]

    def take_all(k, carry):
        p = (me + k) % group
        all_copy(p, p).wait_recv()
        return carry

    lax.fori_loop(1, group, take_all, 0)
    total_ref[...] = all_s[...].astype(F32)

    def sent_near(k, carry):
        p = (me + k) % group
        near_copy(p, me).wait_send()
        all_copy(p, me).wait_send()
        return carry

    lax.fori_loop(1, group, sent_near, 0)
    for to in range(pieces):

        @pl.when(z != to)
        def _():
            far_copy(to, z).wait_send()

    @pl.when(z < pieces)
    def _():
        def sent_fin(k, carry):
            fin_copy((z + k) % depth, z).wait_send()
            return carry

        lax.fori_loop(1, depth, sent_fin, 0)


def full(shape):
    return pl.BlockSpec(shape, lambda *_: (0,) * len(shape))


def chunked(shape):
    return pl.BlockSpec(shape, lambda step, *_: (step,) + (0,) * (len(shape) - 1))


def fine_select():
    row = lax.broadcasted_iota(jnp.int32, (256, 256), 0)
    column = lax.broadcasted_iota(jnp.int32, (256, 256), 1)
    tap, i, j = row // 64, row // 8 % 8, row % 8
    return (column == 16 * (2 * i + tap // 2) + 2 * j + tap % 2).astype(BF16)


def shards(plane, fine, cotangent, counts, parent, quadrant, down_weight, mid_weight, up_weight):
    number = fine.shape[1]
    slots = lax.axis_size("tile")
    events = lax.axis_size("event")
    coarse_dev = number // 4
    rows = number * PIXELS
    steps = number // CHUNK
    step_rows = CHUNK * PIXELS
    scale = 1.0 / math.sqrt(events * slots * number * 64)
    select = fine_select()
    mid_flat = mid_weight.reshape(9 * 128, 128)
    mid_back = jnp.transpose(mid_weight, (0, 2, 1)).reshape(9 * 128, 128)
    scalars = (counts[0], parent[0], quadrant[0])
    fine_tiles, cot_tiles = fine[0], cotangent[0]

    x_taps, g_taps, pre, local, grad_out, up = pl.pallas_call(
        functools.partial(holder_first, coarse_dev),
        grid_spec=pltpu.PrefetchScalarGridSpec(
            num_scalar_prefetch=3,
            grid=(steps,),
            in_specs=[
                chunked((CHUNK, 32, 256)),
                chunked((CHUNK, 32, 256)),
                full((256, 256)),
                full((4, 32, 128)),
                full((4, 32, 128)),
                full((1152, 128)),
            ],
            out_specs=[
                chunked((step_rows // 4, 512)),
                chunked((step_rows // 4, 512)),
                chunked((step_rows, 128)),
                chunked((step_rows, 128)),
                chunked((step_rows, 128)),
                full((slots, UP_ROWS, 128)),
            ],
            scratch_shapes=[
                pltpu.VMEM((512, 512), BF16),
                pltpu.VMEM((512, 512), BF16),
                pltpu.VMEM((step_rows, 1152), BF16),
                pltpu.VMEM((step_rows, 128), F32),
                pltpu.VMEM((step_rows, 128), F32),
            ],
        ),
        out_shape=[
            jax.ShapeDtypeStruct((rows // 4, 512), BF16),
            jax.ShapeDtypeStruct((rows // 4, 512), BF16),
            jax.ShapeDtypeStruct((rows, 128), F32),
            jax.ShapeDtypeStruct((rows, 128), F32),
            jax.ShapeDtypeStruct((rows, 128), BF16),
            jax.ShapeDtypeStruct((slots, UP_ROWS, 128), BF16),
        ],
        compiler_params=pltpu.CompilerParams(vmem_limit_bytes=VMEM_LIMIT),
        name="holder_first",
    )(*scalars, fine_tiles, cot_tiles, select, down_weight, up_weight, mid_flat)

    got = lax.all_to_all(up, "tile", split_axis=0, concat_axis=0, tiled=True)
    tags = got[:, UP_ROWS - 1, 0].astype(jnp.int32)
    smem = pl.BlockSpec(memory_space=pltpu.SMEM)
    vmem = pl.BlockSpec(memory_space=pltpu.VMEM)
    reply, cross = pl.pallas_call(
        owner_edges,
        in_specs=[smem, vmem, vmem, vmem],
        out_specs=[vmem, vmem],
        out_shape=[
            jax.ShapeDtypeStruct((slots, DOWN_ROWS, 128), BF16),
            jax.ShapeDtypeStruct((128, 1152), F32),
        ],
        scratch_shapes=[
            pltpu.VMEM((6, 4, coarse_dev * 8 + 8, 128), F32),
            pltpu.VMEM((4, 4, coarse_dev * 8 + 8, 128), F32),
        ],
        compiler_params=pltpu.CompilerParams(vmem_limit_bytes=VMEM_LIMIT),
        name="owner_edges",
    )(tags, got, mid_flat, mid_back)
    back = lax.all_to_all(reply, "tile", split_axis=0, concat_axis=0, tiled=True)

    group = events * plane
    share = -(-1408 // (group * 16)) * 16
    grad_fine, weights = pl.pallas_call(
        functools.partial(holder_last, coarse_dev, scale),
        grid_spec=pltpu.PrefetchScalarGridSpec(
            num_scalar_prefetch=3,
            grid=(steps,),
            in_specs=[
                chunked((CHUNK, 32, 256)),
                chunked((step_rows // 4, 512)),
                chunked((step_rows // 4, 512)),
                chunked((step_rows, 128)),
                chunked((step_rows, 128)),
                chunked((step_rows, 128)),
                full((slots, DOWN_ROWS, 128)),
                full((128, 1152)),
                full((256, 256)),
                full((4, 32, 128)),
                full((1152, 128)),
            ],
            out_specs=[chunked((CHUNK, 32, 256)), full((group * share, 128))],
            scratch_shapes=[
                pltpu.VMEM((512, 512), BF16),
                pltpu.VMEM((step_rows, 1152), BF16),
                pltpu.VMEM((step_rows, 128), F32),
                pltpu.VMEM((step_rows, 128), F32),
                pltpu.VMEM((128, 1152), F32),
                pltpu.VMEM((512, 512), F32),
                pltpu.VMEM((512, 512), F32),
            ],
        ),
        out_shape=[
            jax.ShapeDtypeStruct((number, 32, 256), BF16),
            jax.ShapeDtypeStruct((group * share, 128), BF16),
        ],
        compiler_params=pltpu.CompilerParams(vmem_limit_bytes=VMEM_LIMIT),
        name="holder_last",
    )(
        *scalars, cot_tiles, x_taps, g_taps, pre, local, grad_out, back, cross, select,
        down_weight, mid_back,
    )

    depth = slots // plane
    pieces = max(n for n in range(1, share // 8 + 1) if share // 8 % n == 0 and n <= depth)
    piece = share // pieces
    dma = pltpu.SemaphoreType.DMA
    total = pl.pallas_call(
        functools.partial(sum_weights, events, plane, depth, pieces),
        in_specs=[vmem],
        out_specs=vmem,
        out_shape=jax.ShapeDtypeStruct((group * share, 128), F32),
        scratch_shapes=[
            pltpu.VMEM((group, share, 128), BF16),
            pltpu.VMEM((pieces, piece, 128), F32),
            pltpu.VMEM((depth, piece, 128), F32),
            pltpu.VMEM((pieces, piece, 128), F32),
            pltpu.VMEM((share, 128), BF16),
            pltpu.VMEM((group * share, 128), BF16),
            dma((group,)),
            dma((group,)),
            dma((pieces,)),
            dma((depth,)),
            dma((depth,)),
            dma((pieces,)),
            dma((group,)),
            dma((group,)),
        ],
        compiler_params=pltpu.CompilerParams(
            collective_id=0, has_side_effects=True, vmem_limit_bytes=VMEM_LIMIT
        ),
        name="sum_weights",
    )(weights)
    return (
        grad_fine[None],
        total[1152:1280].reshape(4, 32, 128),
        total[:1152].reshape(9, 128, 128),
        total[1280:1408].reshape(4, 32, 128),
    )


def solution(mesh):
    placed = (
        P("event", "tile", None, None),
        P("event", "tile", None, None),
        P("event", "tile"),
        P("event", "tile"),
        P("event", "tile"),
        P(),
        P(),
        P(),
    )
    return jax.shard_map(
        functools.partial(shards, 8),
        mesh=mesh,
        in_specs=placed,
        out_specs=(P("event", "tile", None, None), P(), P(), P()),
        check_vma=False,
    )
```

```python
import functools
import math

import jax
import jax.numpy as jnp
from jax import lax
from jax.experimental import pallas as pl
from jax.experimental.pallas import tpu as pltpu
from jax.sharding import PartitionSpec as P

MESH = pl.DeviceIdType.MESH
F32 = jnp.float32
BF16 = jnp.bfloat16
CHUNK = 16
PIXELS = 64
EDGE_ROWS = 16
VMEM_LIMIT = 48 * 1024 * 1024
FIRST_LIMIT = 60 * 1024 * 1024


def mm(a, b):
    return jnp.dot(a, b, preferred_element_type=F32)


def mm_nt(a, b):
    return lax.dot_general(a, b, (((1,), (1,)), ((), ())), preferred_element_type=F32)


def mm_tn(a, b):
    return lax.dot_general(a, b, (((0,), (0,)), ((), ())), preferred_element_type=F32)


def sigmoid(v):
    return 0.5 * jnp.tanh(0.5 * v) + 0.5


def slope(v):
    g = sigmoid(v)
    return g * (1.0 + v * (1.0 - g))


def shift8(x, step, fill=None):
    if step == 0:
        return x
    place = lax.broadcasted_iota(jnp.int32, x.shape, 1)
    moved = pltpu.roll(x, 7 if step > 0 else 1, 1)
    outside = place == (7 if step > 0 else 0)
    if fill is None:
        return jnp.where(outside, 0.0, moved)
    return jnp.where(outside, pltpu.roll(fill, 7 if step > 0 else 1, 1), moved)


def side_steps(x, flip):
    blocks = x.reshape(x.shape[0] // 8, 8, 128)
    parts = [shift8(blocks, 1 - s if flip else s - 1) for s in range(3)]
    return jnp.concatenate([part.reshape(x.shape).astype(BF16) for part in parts], axis=1)


def row_step(x, step):
    if step == 0:
        return x
    blocks = x.reshape(x.shape[0] // PIXELS, 8, 8, 128)
    zero = jnp.zeros((blocks.shape[0], 1, 8, 128), x.dtype)
    if step > 0:
        moved = jnp.concatenate([blocks[:, 1:], zero], axis=1)
    else:
        moved = jnp.concatenate([zero, blocks[:, :7]], axis=1)
    return moved.reshape(x.shape)


def spread_weight(weight_ref, spread_ref):
    spread_ref[...] = jnp.zeros_like(spread_ref)
    for tap in range(4):
        for tile in range(4):
            row = tap * 128 + tile * 32
            spread_ref[row : row + 32, tile * 128 : (tile + 1) * 128] = weight_ref[tap]


def to_lanes(x):
    groups = x.shape[0] // (4 * PIXELS)
    rows = []
    for group in range(groups):
        parts = [
            x[(group * 4 + tile) * PIXELS : (group * 4 + tile + 1) * PIXELS] for tile in range(4)
        ]
        rows.append(jnp.concatenate(parts, axis=1))
    return jnp.concatenate(rows, axis=0)


def to_rows(x):
    groups = x.shape[0] // PIXELS
    parts = []
    for group in range(groups):
        for tile in range(4):
            parts.append(x[group * PIXELS : (group + 1) * PIXELS, tile * 128 : (tile + 1) * 128])
    return jnp.concatenate(parts, axis=0)


def taps_to_lanes(x):
    groups = x.shape[1] // 128
    rows = []
    for group in range(groups):
        parts = [
            x[tap * PIXELS : (tap + 1) * PIXELS, group * 128 : (group + 1) * 128]
            for tap in range(4)
        ]
        rows.append(jnp.concatenate(parts, axis=1))
    return jnp.concatenate(rows, axis=0)


def lanes_to_taps(x):
    groups = x.shape[0] // PIXELS
    columns = []
    for group in range(groups):
        parts = [
            x[group * PIXELS : (group + 1) * PIXELS, tap * 128 : (tap + 1) * 128]
            for tap in range(4)
        ]
        columns.append(jnp.concatenate(parts, axis=0))
    return jnp.concatenate(columns, axis=1)


def fill_select(select_s):
    row = lax.broadcasted_iota(jnp.int32, (256, 256), 0)
    column = lax.broadcasted_iota(jnp.int32, (256, 256), 1)
    tap, i, j = row // 64, row // 8 % 8, row % 8
    meet = column == 16 * (2 * i + tap // 2) + 2 * j + tap % 2
    select_s[...] = jnp.where(meet, 1.0, 0.0).astype(BF16)


def place_of(quad):
    return (1 - quad // 2) * 7, (1 - quad % 2) * 7


def read_edges(source, tile, quad):
    edge_y, edge_x = place_of(quad)
    row = source[pl.ds(pl.multiple_of(tile * PIXELS + 8 * edge_y, 8), 8), :]
    col = source[pl.ds(tile * PIXELS + edge_x, 8, stride=8), :]
    return row, jnp.where(quad >= 2, pltpu.roll(col, 7, 0), col)


def add_edges(target, got_ref, base, coarse_dev, count, parent_ref, quad_ref):
    for tile in range(CHUNK):

        @pl.when(base + tile < count)
        def _():
            owner = parent_ref[base + tile] // coarse_dev
            edge_y, edge_x = place_of(quad_ref[base + tile])
            block = got_ref[owner].astype(F32)
            at_row = pl.ds(pl.multiple_of(tile * PIXELS + 8 * edge_y, 8), 8)
            target[at_row, :] += block[:8]
            at_col = pl.ds(tile * PIXELS + edge_x, 8, stride=8)
            target[at_col, :] += block[8:]


def down_conv(
    coarse_dev, count_ref, parent_ref, quad_ref, fine_ref, down_ref,
    x_ref, pre_ref, act_ref, send_ref, select_s, down_s, act_s,
):
    step = pl.program_id(0)
    base = step * CHUNK
    count = count_ref[0]

    @pl.when(step == 0)
    def _():
        fill_select(select_s)
        spread_weight(down_ref, down_s)
        send_ref[...] = jnp.full(send_ref.shape, -1.0, BF16)

    x_taps = taps_to_lanes(mm_nt(select_s[...], fine_ref[...].reshape(CHUNK * 32, 256)).astype(BF16))
    x_ref[...] = x_taps
    pre = to_rows(mm(x_taps, down_s[...]))
    pre_ref[...] = pre
    act = (pre * sigmoid(pre)).astype(BF16)
    act_ref[...] = act
    act_s[...] = act.astype(F32)
    place = lax.broadcasted_iota(jnp.int32, (8, 128), 0)
    for tile in range(CHUNK):
        parent, quad = parent_ref[base + tile], quad_ref[base + tile]
        owner = parent // coarse_dev
        cell = (parent - owner * coarse_dev) * 4 + quad
        row, col = read_edges(act_s, tile, quad)
        col = jnp.where(place == 7, cell.astype(F32), col)

        @pl.when(base + tile < count)
        def _():
            send_ref[owner] = jnp.concatenate([row, col], axis=0).astype(BF16)


def local_conv(
    count_ref, act_ref, cot_ref, up_ref, mid_ref, g_ref, grad_out_ref, local_ref,
    select_s, up_s, mid_s,
):
    step = pl.program_id(0)

    @pl.when(step == 0)
    def _():
        fill_select(select_s)
        spread_weight(up_ref, up_s)
        for sy in range(3):
            for sx in range(3):
                mid_s[sx * 128 : (sx + 1) * 128, sy * 128 : (sy + 1) * 128] = mid_ref[3 * sy + sx]

    g_taps = mm_nt(select_s[...], cot_ref[...].reshape(CHUNK * 32, 256))
    tile_of = lax.broadcasted_iota(jnp.int32, g_taps.shape, 1) // 32 + step * CHUNK
    g_taps = taps_to_lanes(jnp.where(tile_of < count_ref[0], g_taps, 0.0).astype(BF16))
    g_ref[...] = g_taps
    grad_out_ref[...] = to_rows(mm(g_taps, up_s[...])).astype(BF16)
    parts = mm(side_steps(act_ref[...].astype(F32), False), mid_s[...])
    local_ref[...] = (
        row_step(parts[:, :128], -1) + parts[:, 128:256] + row_step(parts[:, 256:], 1)
    )


def gather_edges(tag_ref, got_ref, edge_s, number):
    def take(slot, carry):
        tag = tag_ref[slot]
        cell = jnp.where(tag < 0, number * 4, tag)
        tile, quad = cell // 4, cell % 4
        block = got_ref[slot].astype(F32)
        at = pl.ds(pl.multiple_of(tile * 8, 8), 8)
        edge_s[0, quad, at, :] = block[:8]
        edge_s[1, quad, at, :] = jnp.where(quad >= 2, pltpu.roll(block[8:], 1, 0), block[8:])
        return carry

    edge_s[...] = jnp.zeros_like(edge_s)
    lax.fori_loop(0, got_ref.shape[0], take, 0, unroll=8)


def scatter_edges(tag_ref, reply_s, send_ref, number):
    def give(slot, carry):
        tag = tag_ref[slot]
        cell = jnp.where(tag < 0, number * 4, tag)
        tile, quad = cell // 4, cell % 4
        at = pl.ds(pl.multiple_of(tile * 8, 8), 8)
        parts = [reply_s[kind, quad, at, :] for kind in range(2)]
        send_ref[slot] = jnp.concatenate(parts, axis=0).astype(BF16)
        return carry

    lax.fori_loop(0, send_ref.shape[0], give, 0, unroll=8)


def corner(x, at):
    return jnp.broadcast_to(x[:, at : at + 1, :], x.shape)


def pack(parts):
    rows = parts[0].shape[0] * 8
    return jnp.concatenate([part.reshape(rows, 128).astype(BF16) for part in parts], axis=1)


def edges_of(edge_s, number):
    rows, cols = [], []
    for quad in range(4):
        at_y, at_x = place_of(quad)
        row = edge_s[0, quad, : number * 8, :].reshape(number, 8, 128)
        col = edge_s[1, quad, : number * 8, :].reshape(number, 8, 128)
        place = lax.broadcasted_iota(jnp.int32, row.shape, 1)
        rows.append(row)
        cols.append(jnp.where(place == at_y, corner(row, at_x), col))
    return rows, cols


def write_reply(reply_s, quad, row, col):
    at_y, at_x = place_of(quad)
    rows = row.shape[0] * 8
    place = lax.broadcasted_iota(jnp.int32, row.shape, 1)
    row = row + jnp.where(place == at_x, corner(col, at_y), 0.0)
    reply_s[0, quad, :rows, :] = row.reshape(rows, 128)
    reply_s[1, quad, :rows, :] = jnp.where(place == at_y, 0.0, col).reshape(rows, 128)


def cross_mid(tag_ref, got_ref, mid_ref, send_ref, act_ref, edge_s, reply_s):
    number = edge_s.shape[2] // 8 - 1
    gather_edges(tag_ref, got_ref, edge_s, number)
    act_row, act_col = edges_of(edge_s, number)
    for quad in range(4):
        low, right = quad // 2, quad % 2
        act_ref[0, quad] = act_row[quad].reshape(number * 8, 128).astype(BF16)
        act_ref[1, quad] = act_col[quad].reshape(number * 8, 128).astype(BF16)
        across, beyond, beside = act_row[quad ^ 2], act_row[quad ^ 3], act_col[quad ^ 1]
        fills = [beyond if right == 1 else None, None, beyond if right == 0 else None]
        sy, sx = 2 - 2 * low, 2 - 2 * right
        patch = pack([shift8(across, s - 1, fills[s]) for s in range(3)])
        weight = jnp.concatenate([mid_ref[3 * sy + s] for s in range(3)], axis=0)
        row = mm(patch, weight).reshape(number, 8, 128)
        patch = pack([shift8(beside, s - 1) for s in range(3)])
        weight = jnp.concatenate([mid_ref[3 * s + sx] for s in range(3)], axis=0)
        col = mm(patch, weight).reshape(number, 8, 128)
        write_reply(reply_s, quad, row, col)
    reply_s[:, :, number * 8 :, :] = jnp.zeros((2, 4, 8, 128), F32)
    scatter_edges(tag_ref, reply_s, send_ref, number)


def cross_grad(tag_ref, got_ref, mid_ref, act_ref, send_ref, cross_ref, edge_s, reply_s):
    number = edge_s.shape[2] // 8 - 1
    gather_edges(tag_ref, got_ref, edge_s, number)
    grad_row, grad_col = edges_of(edge_s, number)
    cross_ref[...] = jnp.zeros_like(cross_ref)
    for quad in range(4):
        low, right = quad // 2, quad % 2
        across, beyond, beside = grad_row[quad ^ 2], grad_row[quad ^ 3], grad_col[quad ^ 1]
        fills = [beyond if right == 0 else None, None, beyond if right == 1 else None]
        sy, sx = 2 * low, 2 * right
        patch = pack([shift8(across, 1 - s, fills[s]) for s in range(3)])
        weight = jnp.concatenate([mid_ref[3 * sy + s] for s in range(3)], axis=1)
        row = mm_nt(patch, weight).reshape(number, 8, 128)
        cross_ref[sy * 128 : (sy + 1) * 128, :] += mm_tn(act_ref[0, quad], patch)
        patch = pack([shift8(beside, 1 - s) for s in range(3)])
        weight = jnp.concatenate([mid_ref[3 * s + sx] for s in range(3)], axis=1)
        col = mm_nt(patch, weight).reshape(number, 8, 128)
        part = mm_tn(act_ref[1, quad], patch)
        for s in range(3):
            cross_ref[s * 128 : (s + 1) * 128, sx * 128 : (sx + 1) * 128] += (
                part[:, s * 128 : (s + 1) * 128]
            )
        write_reply(reply_s, quad, row, col)
    reply_s[:, :, number * 8 :, :] = jnp.zeros((2, 4, 8, 128), F32)
    scatter_edges(tag_ref, reply_s, send_ref, number)


def mid_slopes(
    coarse_dev, count_ref, parent_ref, quad_ref, local_ref, act_ref, grad_out_ref, got_ref,
    out_ref, grad_ref, send_ref, mid_s,
):
    step = pl.program_id(0)
    base = step * CHUNK
    count = count_ref[0]

    @pl.when(step == 0)
    def _():
        send_ref[...] = jnp.zeros(send_ref.shape, BF16)

    mid_s[...] = local_ref[...]
    add_edges(mid_s, got_ref, base, coarse_dev, count, parent_ref, quad_ref)
    mid = mid_s[...]
    gate = sigmoid(mid)
    out_ref[...] = (act_ref[...].astype(F32) + mid * gate).astype(BF16)
    grad = grad_out_ref[...].astype(F32) * (gate * (1.0 + mid * (1.0 - gate)))
    grad = grad.astype(BF16)
    grad_ref[...] = grad
    mid_s[...] = grad.astype(F32)
    for tile in range(CHUNK):
        row, col = read_edges(mid_s, tile, quad_ref[base + tile])

        @pl.when(base + tile < count)
        def _():
            owner = parent_ref[base + tile] // coarse_dev
            send_ref[owner] = jnp.concatenate([row, col], axis=0).astype(BF16)


def local_grads(
    g_ref, out_ref, grad_ref, grad_out_ref, act_ref, mid_ref,
    grad_act_ref, mid_acc, up_ref, up_acc, mid_s,
):
    step = pl.program_id(0)

    @pl.when(step == 0)
    def _():
        mid_acc[...] = jnp.zeros_like(mid_acc)
        up_acc[...] = jnp.zeros_like(up_acc)
        for sy in range(3):
            for sx in range(3):
                mid_s[sy * 128 : (sy + 1) * 128, sx * 128 : (sx + 1) * 128] = mid_ref[3 * sy + sx]

    up_acc[...] += mm_tn(g_ref[...], to_lanes(out_ref[...]))
    steps = side_steps(grad_ref[...].astype(F32), True)
    parts = mm_nt(steps, mid_s[...])
    grad_act_ref[...] = (
        grad_out_ref[...].astype(F32)
        + row_step(parts[:, :128], 1)
        + parts[:, 128:256]
        + row_step(parts[:, 256:], -1)
    )
    act = act_ref[...].astype(F32)
    acts = jnp.concatenate([row_step(act, s - 1).astype(BF16) for s in range(3)], axis=1)
    mid_acc[...] += mm_tn(acts, steps)

    @pl.when(step == pl.num_programs(0) - 1)
    def _():
        fold_taps(up_acc, up_ref)


def fold_taps(acc, out_ref):
    for tap in range(4):
        part = jnp.zeros((32, 128), F32)
        for tile in range(4):
            row = tap * 128 + tile * 32
            part += acc[row : row + 32, tile * 128 : (tile + 1) * 128]
        out_ref[tap * 32 : (tap + 1) * 32, :] = part


def fine_grads(
    coarse_dev, count_ref, parent_ref, quad_ref, cot_ref, x_ref, pre_ref, grad_act_ref, got_ref,
    down_ref, fine_ref, sum_ref, select_s, down_s, act_s, down_acc,
):
    step = pl.program_id(0)
    base = step * CHUNK
    count = count_ref[0]

    @pl.when(step == 0)
    def _():
        fill_select(select_s)
        spread_weight(down_ref, down_s)
        down_acc[...] = jnp.zeros_like(down_acc)

    act_s[...] = grad_act_ref[...]
    add_edges(act_s, got_ref, base, coarse_dev, count, parent_ref, quad_ref)
    grad_act = act_s[...].astype(BF16).astype(F32)
    grad_pre = to_lanes((grad_act * slope(pre_ref[...])).astype(BF16))
    down_acc[...] += mm_tn(x_ref[...], grad_pre)
    back = lanes_to_taps(mm_nt(grad_pre, down_s[...]))
    high = back.astype(BF16)
    rest = (back - high.astype(F32)).astype(BF16)
    select = select_s[...]
    total = mm_tn(high, select) + mm_tn(rest, select)
    total += cot_ref[...].reshape(CHUNK * 32, 256).astype(F32)
    tile_of = lax.broadcasted_iota(jnp.int32, total.shape, 0) // 32 + base
    total = jnp.where(tile_of < count, total, 0.0)
    fine_ref[...] = total.astype(BF16).reshape(CHUNK, 32, 256)

    @pl.when(step == pl.num_programs(0) - 1)
    def _():
        fold_taps(down_acc, sum_ref)


def sum_weights(
    events, plane, depth, pieces, scale, local_ref, cross_ref, up_ref, mid_ref, grad_up_ref,
    mine_ref, near_s, sum_s, far_s, fin_s, low_s, all_s,
    near_send, near_recv, far_send, far_recv, fin_send, fin_recv, all_send, all_recv,
):
    event = lax.axis_index("event")
    tile = lax.axis_index("tile")
    z = tile // plane
    low = tile % plane
    group = events * plane
    me = event * plane + low
    share = mine_ref.shape[0] // group
    piece = share // pieces
    for tap in range(9):
        at = slice(tap // 3 * 128, tap // 3 * 128 + 128), slice(tap % 3 * 128, tap % 3 * 128 + 128)
        mine_ref[tap * 128 : (tap + 1) * 128, :] = (
            (local_ref[at] + cross_ref[at]) * scale
        ).astype(BF16)
    mine_ref[1152:1280, :] = (up_ref[...] * scale).astype(BF16)
    if mine_ref.shape[0] > 1280:
        mine_ref[1280:, :] = jnp.zeros((mine_ref.shape[0] - 1280, 128), BF16)

    def near_id(p):
        return (p // plane, z * plane + p % plane)

    def far_id(p):
        return (event, p * plane + low)

    barrier = pltpu.get_barrier_semaphore()

    def greet_near(k, carry):
        pl.semaphore_signal(
            barrier, inc=1, device_id=near_id((me + k) % group), device_id_type=MESH
        )
        return carry

    def greet_far(k, carry):
        pl.semaphore_signal(
            barrier, inc=1, device_id=far_id((z + k) % depth), device_id_type=MESH
        )
        return carry

    lax.fori_loop(1, group, greet_near, 0)
    lax.fori_loop(1, depth, greet_far, 0)
    pl.semaphore_wait(barrier, group + depth - 2)

    def rows(p):
        return pl.ds(pl.multiple_of(p * share, 16), share)

    def near_copy(to, slot):
        return pltpu.make_async_remote_copy(
            src_ref=mine_ref.at[rows(to)],
            dst_ref=near_s.at[slot],
            send_sem=near_send.at[to],
            recv_sem=near_recv.at[slot],
            device_id=near_id(to),
            device_id_type=MESH,
        )

    def send_near(k, carry):
        near_copy((me + k) % group, me).start()
        return carry

    lax.fori_loop(1, group, send_near, 0)

    def take_near(k, total):
        p = (me + k) % group
        near_copy(p, p).wait_recv()
        return total + near_s[p].astype(F32)

    total = lax.fori_loop(1, group, take_near, mine_ref[rows(me), :].astype(F32))
    sum_s[...] = total.reshape(pieces, piece, 128)

    def far_copy(to, slot):
        return pltpu.make_async_remote_copy(
            src_ref=sum_s.at[to],
            dst_ref=far_s.at[slot],
            send_sem=far_send.at[to],
            recv_sem=far_recv.at[slot],
            device_id=far_id(to),
            device_id_type=MESH,
        )

    for to in range(pieces):

        @pl.when(z != to)
        def _():
            far_copy(to, z).start()

    def fin_copy(to, slot):
        return pltpu.make_async_remote_copy(
            src_ref=fin_s.at[slot],
            dst_ref=fin_s.at[slot],
            send_sem=fin_send.at[to],
            recv_sem=fin_recv.at[slot],
            device_id=far_id(to),
            device_id_type=MESH,
        )

    @pl.when(z < pieces)
    def _():
        def take_far(k, total):
            p = (z + k) % depth
            far_copy(z, p).wait_recv()
            return total + far_s[p]

        fin_s[z] = lax.fori_loop(1, depth, take_far, sum_s[z])

        def send_fin(k, carry):
            fin_copy((z + k) % depth, z).start()
            return carry

        lax.fori_loop(1, depth, send_fin, 0)

    for p in range(pieces):

        @pl.when(z != p)
        def _():
            fin_copy(p, p).wait_recv()

    low_s[...] = fin_s[...].reshape(share, 128).astype(BF16)

    def all_copy(to, slot):
        return pltpu.make_async_remote_copy(
            src_ref=low_s,
            dst_ref=all_s.at[rows(slot)],
            send_sem=all_send.at[to],
            recv_sem=all_recv.at[slot],
            device_id=near_id(to),
            device_id_type=MESH,
        )

    def send_all(k, carry):
        all_copy((me + k) % group, me).start()
        return carry

    lax.fori_loop(1, group, send_all, 0)
    all_s[rows(me), :] = low_s[...]

    def take_all(k, carry):
        p = (me + k) % group
        all_copy(p, p).wait_recv()
        return carry

    lax.fori_loop(1, group, take_all, 0)
    mid_ref[...] = all_s[:1152, :].astype(F32)
    grad_up_ref[...] = all_s[1152:1280, :].astype(F32)

    def sent_near(k, carry):
        p = (me + k) % group
        near_copy(p, me).wait_send()
        all_copy(p, me).wait_send()
        return carry

    lax.fori_loop(1, group, sent_near, 0)
    for to in range(pieces):

        @pl.when(z != to)
        def _():
            far_copy(to, z).wait_send()

    @pl.when(z < pieces)
    def _():
        def sent_fin(k, carry):
            fin_copy((z + k) % depth, z).wait_send()
            return carry

        lax.fori_loop(1, depth, sent_fin, 0)


def sum_down(
    events, plane, depth, scale, mine_ref, total_ref, mine_s, near_s, low_s, far_s, fin_s, all_s,
    near_send, near_recv, far_send, far_recv, all_send, all_recv,
):
    event = lax.axis_index("event")
    tile = lax.axis_index("tile")
    z = tile // plane
    group = events * plane
    me = event * plane + tile % plane
    pieces = mine_ref.shape[0] // 16
    stride = group // pieces
    my_piece = me // stride
    reducer = me % stride == 0

    def near_id(p):
        return (p // plane, z * plane + p % plane)

    def far_id(p):
        return (event, p * plane + tile % plane)

    barrier = pltpu.get_barrier_semaphore()

    def greet(to):
        pl.semaphore_signal(barrier, inc=1, device_id=to, device_id_type=MESH)

    @pl.when(reducer)
    def _():
        def near(k, carry):
            greet(near_id((me + k) % group))
            return carry

        def far(k, carry):
            greet(far_id((z + k) % depth))
            return carry

        lax.fori_loop(1, group, near, 0)
        lax.fori_loop(1, depth, far, 0)

    @pl.when(me % stride != 0)
    def _():
        for p in range(pieces):
            greet(near_id(p * stride))

    mine_s[...] = (mine_ref[...] * scale).astype(BF16).reshape(mine_s.shape)

    @pl.when(reducer)
    def _():
        pl.semaphore_wait(barrier, group + depth - 2)

    @pl.when(me % stride != 0)
    def _():
        pl.semaphore_wait(barrier, pieces)

    def near_copy(piece, slot):
        return pltpu.make_async_remote_copy(
            src_ref=mine_s.at[piece],
            dst_ref=near_s.at[slot],
            send_sem=near_send.at[piece],
            recv_sem=near_recv.at[slot],
            device_id=near_id(piece * stride),
            device_id_type=MESH,
        )

    def far_copy(to, slot):
        return pltpu.make_async_remote_copy(
            src_ref=low_s,
            dst_ref=far_s.at[slot],
            send_sem=far_send.at[to],
            recv_sem=far_recv.at[slot],
            device_id=far_id(to),
            device_id_type=MESH,
        )

    def all_copy(to, piece):
        return pltpu.make_async_remote_copy(
            src_ref=fin_s,
            dst_ref=all_s.at[piece],
            send_sem=all_send.at[to],
            recv_sem=all_recv.at[piece],
            device_id=near_id(to),
            device_id_type=MESH,
        )

    for piece in range(pieces):

        @pl.when(me != piece * stride)
        def _():
            near_copy(piece, me).start()

    @pl.when(reducer)
    def _():
        def take_near(k, total):
            p = (me + k) % group
            near_copy(my_piece, p).wait_recv()
            return total + near_s[p].astype(F32)

        total = lax.fori_loop(1, group, take_near, mine_s[my_piece].astype(F32))
        low_s[...] = total.astype(BF16)

        def send_far(k, carry):
            far_copy((z + k) % depth, z).start()
            return carry

        lax.fori_loop(1, depth, send_far, 0)
        far_s[z] = low_s[...]

        def take_far(k, carry):
            p = (z + k) % depth
            far_copy(p, p).wait_recv()
            return carry

        lax.fori_loop(1, depth, take_far, 0)
        final = jnp.sum(far_s[...].astype(F32), axis=0)
        fin_s[...] = final.astype(BF16)

        def send_all(k, carry):
            all_copy((me + k) % group, my_piece).start()
            return carry

        lax.fori_loop(1, group, send_all, 0)
        all_s[my_piece] = fin_s[...]

    for piece in range(pieces):

        @pl.when(me != piece * stride)
        def _():
            all_copy(me, piece).wait_recv()

    total_ref[...] = all_s[...].reshape(total_ref.shape).astype(F32)
    for piece in range(pieces):

        @pl.when(me != piece * stride)
        def _():
            near_copy(piece, me).wait_send()

    @pl.when(reducer)
    def _():
        def sent_far(k, carry):
            far_copy((z + k) % depth, z).wait_send()
            return carry

        def sent_all(k, carry):
            all_copy((me + k) % group, my_piece).wait_send()
            return carry

        lax.fori_loop(1, depth, sent_far, 0)
        lax.fori_loop(1, group, sent_all, 0)


def full(shape):
    return pl.BlockSpec(shape, lambda *_: (0,) * len(shape))


def chunked(shape):
    return pl.BlockSpec(shape, lambda step, *_: (step,) + (0,) * (len(shape) - 1))


def like(shape, dtype):
    return jax.ShapeDtypeStruct(shape, dtype)


def gridded(body, name, steps, scalars, arrays, in_specs, outs, scratch, flops, limit=VMEM_LIMIT):
    return pl.pallas_call(
        body,
        grid_spec=pltpu.PrefetchScalarGridSpec(
            num_scalar_prefetch=len(scalars),
            grid=(steps,),
            in_specs=in_specs,
            out_specs=[spec for spec, _ in outs],
            scratch_shapes=scratch,
        ),
        out_shape=[shape for _, shape in outs],
        compiler_params=pltpu.CompilerParams(vmem_limit_bytes=limit),
        cost_estimate=pl.CostEstimate(
            flops=flops, bytes_accessed=8 * 1024 * 1024, transcendentals=0
        ),
        name=name,
    )(*scalars, *arrays)


def whole(body, name, arrays, in_specs, outs, scratch, collective=None):
    params = dict(vmem_limit_bytes=VMEM_LIMIT)
    if collective is not None:
        params.update(collective_id=collective, has_side_effects=True)
    vmem = pl.BlockSpec(memory_space=pltpu.VMEM)
    return pl.pallas_call(
        body,
        in_specs=in_specs,
        out_specs=[vmem] * len(outs),
        out_shape=outs,
        scratch_shapes=scratch,
        compiler_params=pltpu.CompilerParams(**params),
        cost_estimate=pl.CostEstimate(
            flops=4 * 10**9, bytes_accessed=4 * 1024 * 1024, transcendentals=0
        ),
        name=name,
    )(*arrays)


def exchange(x):
    return lax.all_to_all(x, "tile", split_axis=0, concat_axis=0, tiled=True)


def shards(plane, fine, cotangent, counts, parent, quadrant, down_weight, mid_weight, up_weight):
    number = fine.shape[1]
    slots = lax.axis_size("tile")
    events = lax.axis_size("event")
    coarse_dev = number // 4
    rows = number * PIXELS
    steps = number // CHUNK
    step_rows = CHUNK * PIXELS
    scale = 1.0 / math.sqrt(events * slots * number * 64)
    scalars = (counts[0], parent[0], quadrant[0])
    message = like((slots, EDGE_ROWS, 128), BF16)
    messages = full((slots, EDGE_ROWS, 128))
    tiles = chunked((CHUNK, 32, 256))
    taps = chunked((step_rows // 4, 512))
    pixels = chunked((step_rows, 128))
    taps_shape = like((rows // 4, 512), BF16)
    wide, narrow = like((rows, 128), F32), like((rows, 128), BF16)
    thin, square = full((4, 32, 128)), full((9, 128, 128))
    smem = pl.BlockSpec(memory_space=pltpu.SMEM)
    vmem = pl.BlockSpec(memory_space=pltpu.VMEM)
    spread = pltpu.VMEM((512, 512), BF16)
    nine = pltpu.VMEM((384, 384), BF16)
    pixel_s = pltpu.VMEM((step_rows, 128), F32)
    select_s = pltpu.VMEM((256, 256), BF16)
    edge_s = pltpu.VMEM((2, 4, coarse_dev * 8 + 8, 128), F32)
    edges = like((2, 4, coarse_dev * 8, 128), BF16)

    x_taps, pre, act, act_edges = gridded(
        functools.partial(down_conv, coarse_dev),
        "down_conv",
        steps,
        scalars,
        (fine[0], down_weight),
        [tiles, thin],
        [(taps, taps_shape), (pixels, wide), (pixels, narrow), (messages, message)],
        [select_s, spread, pixel_s],
        10**9,
        FIRST_LIMIT,
    )
    got = exchange(act_edges)
    g_taps, grad_out, local = gridded(
        local_conv,
        "local_conv",
        steps,
        scalars[:1],
        (act, cotangent[0], up_weight, mid_weight),
        [pixels, tiles, thin, square],
        [(taps, taps_shape), (pixels, narrow), (pixels, wide)],
        [select_s, spread, nine],
        4 * 10**9,
    )
    tags = got[:, EDGE_ROWS - 1, 0].astype(jnp.int32)
    reply, act_edges = whole(
        cross_mid, "cross_mid", (tags, got, mid_weight), [smem, vmem, vmem],
        [message, edges], [edge_s, edge_s],
    )
    got = exchange(reply)
    out, grad, grad_edges = gridded(
        functools.partial(mid_slopes, coarse_dev),
        "mid_slopes",
        steps,
        scalars,
        (local, act, grad_out, got),
        [pixels, pixels, pixels, messages],
        [(pixels, narrow), (pixels, narrow), (messages, message)],
        [pixel_s],
        10**9,
    )
    got = exchange(grad_edges)
    grad_act, grad_mid, grad_up = gridded(
        local_grads,
        "local_grads",
        steps,
        (),
        (g_taps, out, grad, grad_out, act, mid_weight),
        [taps, pixels, pixels, pixels, pixels, square],
        [
            (pixels, wide),
            (full((384, 384)), like((384, 384), F32)),
            (full((128, 128)), like((128, 128), F32)),
        ],
        [pltpu.VMEM((512, 512), F32), nine],
        6 * 10**9,
    )
    reply, cross = whole(
        cross_grad, "cross_grad", (tags, got, mid_weight, act_edges), [smem, vmem, vmem, vmem],
        [message, like((384, 384), F32)], [edge_s, edge_s],
    )
    got = exchange(reply)

    group = events * plane
    depth = slots // plane
    share = -(-1280 // (group * 16)) * 16
    pieces = max(n for n in range(1, share // 8 + 1) if share // 8 % n == 0 and n <= depth)
    piece = share // pieces
    dma = pltpu.SemaphoreType.DMA
    grad_mid, grad_up = whole(
        functools.partial(sum_weights, events, plane, depth, pieces, scale),
        "sum_weights",
        (grad_mid, cross, grad_up),
        [vmem] * 3,
        [like((1152, 128), F32), like((128, 128), F32)],
        [
            pltpu.VMEM((group * share, 128), BF16),
            pltpu.VMEM((group, share, 128), BF16),
            pltpu.VMEM((pieces, piece, 128), F32),
            pltpu.VMEM((depth, piece, 128), F32),
            pltpu.VMEM((pieces, piece, 128), F32),
            pltpu.VMEM((share, 128), BF16),
            pltpu.VMEM((group * share, 128), BF16),
            dma((group,)),
            dma((group,)),
            dma((pieces,)),
            dma((depth,)),
            dma((depth,)),
            dma((pieces,)),
            dma((group,)),
            dma((group,)),
        ],
        0,
    )
    grad_fine, grad_down = gridded(
        functools.partial(fine_grads, coarse_dev),
        "fine_grads",
        steps,
        scalars,
        (cotangent[0], x_taps, pre, grad_act, got, down_weight),
        [tiles, taps, pixels, pixels, messages, thin],
        [(tiles, like((number, 32, 256), BF16)), (full((128, 128)), like((128, 128), F32))],
        [select_s, spread, pixel_s, pltpu.VMEM((512, 512), F32)],
        4 * 10**9,
    )
    (grad_down,) = whole(
        functools.partial(sum_down, events, plane, depth, scale),
        "sum_down",
        (grad_down,),
        [vmem],
        [like((128, 128), F32)],
        [
            pltpu.VMEM((8, 16, 128), BF16),
            pltpu.VMEM((group, 16, 128), BF16),
            pltpu.VMEM((16, 128), BF16),
            pltpu.VMEM((depth, 16, 128), BF16),
            pltpu.VMEM((16, 128), BF16),
            pltpu.VMEM((8, 16, 128), BF16),
            dma((8,)),
            dma((group,)),
            dma((depth,)),
            dma((depth,)),
            dma((group,)),
            dma((8,)),
        ],
        1,
    )
    return (
        grad_fine[None],
        grad_down.reshape(4, 32, 128),
        grad_mid.reshape(9, 128, 128),
        grad_up.reshape(4, 32, 128),
    )


def solution(mesh):
    placed = (
        P("event", "tile", None, None),
        P("event", "tile", None, None),
        P("event", "tile"),
        P("event", "tile"),
        P("event", "tile"),
        P(),
        P(),
        P(),
    )
    return jax.shard_map(
        functools.partial(shards, 8),
        mesh=mesh,
        in_specs=placed,
        out_specs=(P("event", "tile", None, None), P(), P(), P()),
        check_vma=False,
    )
```

```python
import functools
import math

import jax
import jax.numpy as jnp
from jax import lax
from jax.experimental import pallas as pl
from jax.experimental.pallas import tpu as pltpu
from jax.sharding import PartitionSpec as P

MESH = pl.DeviceIdType.MESH
F32 = jnp.float32
BF16 = jnp.bfloat16
CHUNK = 16
PIXELS = 64
EDGE_ROWS = 16
VMEM_LIMIT = 60 * 1024 * 1024


def mm(a, b):
    return jnp.dot(a, b, preferred_element_type=F32)


def mm_nt(a, b):
    return lax.dot_general(a, b, (((1,), (1,)), ((), ())), preferred_element_type=F32)


def mm_tn(a, b):
    return lax.dot_general(a, b, (((0,), (0,)), ((), ())), preferred_element_type=F32)


def sigmoid(v):
    return 0.5 * jnp.tanh(0.5 * v) + 0.5


def slope(v):
    g = sigmoid(v)
    return g * (1.0 + v * (1.0 - g))


def shift8(x, step, fill=None):
    if step == 0:
        return x
    place = lax.broadcasted_iota(jnp.int32, x.shape, 1)
    moved = pltpu.roll(x, 7 if step > 0 else 1, 1)
    outside = place == (7 if step > 0 else 0)
    if fill is None:
        return jnp.where(outside, 0.0, moved)
    return jnp.where(outside, pltpu.roll(fill, 7 if step > 0 else 1, 1), moved)


def side_steps(x, flip):
    blocks = x.reshape(x.shape[0] // 8, 8, 128)
    parts = [shift8(blocks, 1 - s if flip else s - 1) for s in range(3)]
    return jnp.concatenate([part.reshape(x.shape).astype(BF16) for part in parts], axis=1)


def row_step(x, step):
    if step == 0:
        return x
    blocks = x.reshape(x.shape[0] // PIXELS, 8, 8, 128)
    zero = jnp.zeros((blocks.shape[0], 1, 8, 128), x.dtype)
    if step > 0:
        moved = jnp.concatenate([blocks[:, 1:], zero], axis=1)
    else:
        moved = jnp.concatenate([zero, blocks[:, :7]], axis=1)
    return moved.reshape(x.shape)


def spread_weight(weight_ref, spread_ref):
    spread_ref[...] = jnp.zeros_like(spread_ref)
    for tap in range(4):
        for tile in range(4):
            row = tap * 128 + tile * 32
            spread_ref[row : row + 32, tile * 128 : (tile + 1) * 128] = weight_ref[tap]


def to_lanes(x):
    groups = x.shape[0] // (4 * PIXELS)
    rows = []
    for group in range(groups):
        parts = [
            x[(group * 4 + tile) * PIXELS : (group * 4 + tile + 1) * PIXELS] for tile in range(4)
        ]
        rows.append(jnp.concatenate(parts, axis=1))
    return jnp.concatenate(rows, axis=0)


def to_rows(x):
    groups = x.shape[0] // PIXELS
    parts = []
    for group in range(groups):
        for tile in range(4):
            parts.append(x[group * PIXELS : (group + 1) * PIXELS, tile * 128 : (tile + 1) * 128])
    return jnp.concatenate(parts, axis=0)


def taps_to_lanes(x):
    groups = x.shape[1] // 128
    rows = []
    for group in range(groups):
        parts = [
            x[tap * PIXELS : (tap + 1) * PIXELS, group * 128 : (group + 1) * 128]
            for tap in range(4)
        ]
        rows.append(jnp.concatenate(parts, axis=1))
    return jnp.concatenate(rows, axis=0)


def lanes_to_taps(x):
    groups = x.shape[0] // PIXELS
    columns = []
    for group in range(groups):
        parts = [
            x[group * PIXELS : (group + 1) * PIXELS, tap * 128 : (tap + 1) * 128]
            for tap in range(4)
        ]
        columns.append(jnp.concatenate(parts, axis=0))
    return jnp.concatenate(columns, axis=1)


def fill_select(select_s):
    row = lax.broadcasted_iota(jnp.int32, (256, 256), 0)
    column = lax.broadcasted_iota(jnp.int32, (256, 256), 1)
    tap, i, j = row // 64, row // 8 % 8, row % 8
    meet = column == 16 * (2 * i + tap // 2) + 2 * j + tap % 2
    select_s[...] = jnp.where(meet, 1.0, 0.0).astype(BF16)


def place_of(quad):
    return (1 - quad // 2) * 7, (1 - quad % 2) * 7


def corner(x, at):
    return jnp.broadcast_to(x[:, at : at + 1, :], x.shape)


def pack(parts):
    rows = parts[0].shape[0] * 8
    return jnp.concatenate([part.reshape(rows, 128).astype(BF16) for part in parts], axis=1)


def edges_of(edge_s, number):
    rows, cols = [], []
    for quad in range(4):
        at_y, at_x = place_of(quad)
        row = edge_s[0, quad, : number * 8, :].reshape(number, 8, 128)
        col = edge_s[1, quad, : number * 8, :].reshape(number, 8, 128)
        place = lax.broadcasted_iota(jnp.int32, row.shape, 1)
        rows.append(row)
        cols.append(jnp.where(place == at_y, corner(row, at_x), col))
    return rows, cols


def write_reply(reply_s, quad, row, col):
    at_y, at_x = place_of(quad)
    rows = row.shape[0] * 8
    place = lax.broadcasted_iota(jnp.int32, row.shape, 1)
    row = row + jnp.where(place == at_x, corner(col, at_y), 0.0)
    reply_s[0, quad, :rows, :] = row.reshape(rows, 128)
    reply_s[1, quad, :rows, :] = jnp.where(place == at_y, 0.0, col).reshape(rows, 128)


def fold_taps(acc):
    taps = []
    for tap in range(4):
        part = jnp.zeros((32, 128), F32)
        for tile in range(4):
            row = tap * 128 + tile * 32
            part += acc[row : row + 32, tile * 128 : (tile + 1) * 128]
        taps.append(part)
    return jnp.concatenate(taps, axis=0)


def rows_at(step, size):
    return pl.ds(pl.multiple_of(step * size, size), size)


def side_of(ref, tile):
    return jnp.broadcast_to(ref[pl.ds(tile, 1), :], (8, 128))


def read_edges(value_s, low_ref, right_ref, cell_ref, edges_s, step):
    place = lax.broadcasted_iota(jnp.int32, (8, 128), 0)
    for index in range(CHUNK):
        tile = step * CHUNK + index
        start = pl.multiple_of(tile * PIXELS, PIXELS)
        low, right = side_of(low_ref, tile), side_of(right_ref, tile)
        top = value_s[pl.ds(start, 8), :]
        bottom = value_s[pl.ds(start + 56, 8), :]
        left = value_s[pl.ds(start, 8, stride=8), :]
        end = value_s[pl.ds(start + 7, 8, stride=8), :]
        row = bottom * (1.0 - low) + top * low
        col = end * (1.0 - right) + left * right
        col = col * (1.0 - low) + pltpu.roll(col, 7, 0) * low
        if cell_ref is not None:
            col = jnp.where(place == 7, side_of(cell_ref, tile), col)
        at = pl.ds(pl.multiple_of(tile * EDGE_ROWS, EDGE_ROWS), EDGE_ROWS)
        edges_s[at, :] = jnp.concatenate([row, col], axis=0).astype(BF16)


def fill_holder_routes(owner_ref, hold_s, slots):
    columns = hold_s.shape[1]
    column = lax.broadcasted_iota(jnp.int32, (EDGE_ROWS, columns), 1)
    row = lax.broadcasted_iota(jnp.int32, (EDGE_ROWS, columns), 0)
    here = jnp.where(row == column % EDGE_ROWS, 1.0, 0.0)
    owner = jnp.broadcast_to(owner_ref[...], (EDGE_ROWS, columns))

    def one(slot, carry):
        at = pl.ds(pl.multiple_of(slot * EDGE_ROWS, EDGE_ROWS), EDGE_ROWS)
        hold_s[at, :] = jnp.where(owner == slot.astype(F32), here, 0.0).astype(BF16)
        return carry

    lax.fori_loop(0, slots, one, 0, unroll=2)


def fill_routes(got_ref, route_s):
    slots, columns = got_ref.shape[0], route_s.shape[1]
    column = lax.broadcasted_iota(jnp.int32, (EDGE_ROWS, columns), 1)
    row = lax.broadcasted_iota(jnp.int32, (EDGE_ROWS, columns), 0)
    kind, rest = column // (columns // 2), column % (columns // 2)
    quad, rest = rest // (columns // 8), rest % (columns // 8)
    tile, place = rest // 8, rest % 8
    turned = jnp.where((kind == 1) & (quad >= 2), (place + 7) % 8, place)
    here = jnp.where(row == kind * 8 + turned, 1.0, 0.0)
    cell = (tile * 4 + quad + 1).astype(F32)

    def one(slot, carry):
        tag = got_ref[slot].astype(F32)[EDGE_ROWS - 1 :]
        tag = jnp.concatenate([jnp.broadcast_to(tag, (EDGE_ROWS, 128))] * (columns // 128), axis=1)
        at = pl.ds(pl.multiple_of(slot * EDGE_ROWS, EDGE_ROWS), EDGE_ROWS)
        route_s[at, :] = jnp.where(tag == cell, here, 0.0).astype(BF16)
        return carry

    lax.fori_loop(0, slots, one, 0, unroll=2)


def gather_edges(route_s, got_ref, edge_s):
    rows = got_ref.shape[0] * EDGE_ROWS
    turned = mm_tn(got_ref[...].reshape(rows, 128), route_s[...])
    edge_s[...] = turned.T.reshape(edge_s.shape)


def scatter_edges(route_s, reply_s, send_ref):
    flat = reply_s[...].reshape(route_s.shape[1], 128).astype(BF16)
    send_ref[...] = mm(route_s[...], flat).astype(BF16).reshape(send_ref.shape)


def send_edges(hold_s, edges_s, send_ref):
    send_ref[...] = mm(hold_s[...], edges_s[...]).astype(BF16).reshape(send_ref.shape)


def take_reply(hold_s, got_ref, reply_in_s):
    rows = got_ref.shape[0] * EDGE_ROWS
    reply_in_s[...] = mm_tn(got_ref[...].reshape(rows, 128), hold_s[...]).T


def cross_mid(mid_ref, edge_s, act_edge_s, reply_s):
    number = edge_s.shape[2] // 8
    act_row, act_col = edges_of(edge_s, number)
    for quad in range(4):
        low, right = quad // 2, quad % 2
        act_edge_s[0, quad] = act_row[quad].reshape(number * 8, 128).astype(BF16)
        act_edge_s[1, quad] = act_col[quad].reshape(number * 8, 128).astype(BF16)
        across, beyond, beside = act_row[quad ^ 2], act_row[quad ^ 3], act_col[quad ^ 1]
        fills = [beyond if right == 1 else None, None, beyond if right == 0 else None]
        sy, sx = 2 - 2 * low, 2 - 2 * right
        patch = pack([shift8(across, s - 1, fills[s]) for s in range(3)])
        weight = jnp.concatenate([mid_ref[3 * sy + s] for s in range(3)], axis=0)
        row = mm(patch, weight).reshape(number, 8, 128)
        patch = pack([shift8(beside, s - 1) for s in range(3)])
        weight = jnp.concatenate([mid_ref[3 * s + sx] for s in range(3)], axis=0)
        col = mm(patch, weight).reshape(number, 8, 128)
        write_reply(reply_s, quad, row, col)


def cross_grad(mid_ref, edge_s, act_edge_s, reply_s, cross_ref):
    number = edge_s.shape[2] // 8
    grad_row, grad_col = edges_of(edge_s, number)
    for quad in range(4):
        low, right = quad // 2, quad % 2
        across, beyond, beside = grad_row[quad ^ 2], grad_row[quad ^ 3], grad_col[quad ^ 1]
        fills = [beyond if right == 0 else None, None, beyond if right == 1 else None]
        sy, sx = 2 * low, 2 * right
        patch = pack([shift8(across, 1 - s, fills[s]) for s in range(3)])
        weight = jnp.concatenate([mid_ref[3 * sy + s] for s in range(3)], axis=1)
        row = mm_nt(patch, weight).reshape(number, 8, 128)
        cross_ref[sy * 128 : (sy + 1) * 128, :] += mm_tn(act_edge_s[0, quad], patch)
        patch = pack([shift8(beside, 1 - s) for s in range(3)])
        weight = jnp.concatenate([mid_ref[3 * s + sx] for s in range(3)], axis=1)
        col = mm_nt(patch, weight).reshape(number, 8, 128)
        part = mm_tn(act_edge_s[1, quad], patch)
        for s in range(3):
            cross_ref[s * 128 : (s + 1) * 128, sx * 128 : (sx + 1) * 128] += (
                part[:, s * 128 : (s + 1) * 128]
            )
        write_reply(reply_s, quad, row, col)


def foreign(low_ref, right_ref, reply_in_s, step):
    place = lax.broadcasted_iota(jnp.int32, (8, 128), 0)
    parts = []
    for index in range(CHUNK):
        tile = step * CHUNK + index
        start = pl.multiple_of(tile * EDGE_ROWS, EDGE_ROWS)
        low, right = side_of(low_ref, tile), side_of(right_ref, tile)
        row = reply_in_s[pl.ds(start, 8), :]
        col = reply_in_s[pl.ds(start + 8, 8), :]
        col = col * (1.0 - low) + pltpu.roll(col, 1, 0) * low
        mask = jnp.where(place == 0, right, jnp.where(place == 7, 1.0 - right, 0.0))
        for i in range(8):
            part = mask * jnp.broadcast_to(col[i : i + 1], (8, 128))
            if i == 0:
                part += row * low
            elif i == 7:
                part += row * (1.0 - low)
            parts.append(part)
    return jnp.concatenate(parts, axis=0)


def block(
    events, plane, slots, pieces, scale,
    owner_ref, shown_ref, low_ref, right_ref, cell_ref, active_ref, fine_ref, cot_ref, down_ref, mid_ref, up_ref,
    grad_fine_ref, grad_down_ref, grad_mid_ref, grad_up_ref,
    select_s, down_s, up_s, conv_s, back_s, hold_s, edges_s, reply_in_s,
    x_s, g_s, pre_s, act_s, value_s, mid_s, grad_out_s, out_s,
    send0_s, send1_s, send2_s, send3_s, got0_s, got1_s, got2_s, got3_s, route_s, edge_s, act_edge_s, reply_s,
    mid_acc, up_acc, down_acc,
    mine_s, near_s, sum_s, far_s, fin_s, low_s, all_s,
    mine2_s, near2_s, low2_s, far2_s, fin2_s, all2_s,
    swap_send, swap_recv,
    near_send, near_recv, far_send, far_recv, fin_send, fin_recv, all_send, all_recv,
    near2_send, near2_recv, far2_send, far2_recv, all2_send, all2_recv,
):
    number = fine_ref.shape[0]
    steps = number // CHUNK
    step_rows = CHUNK * PIXELS
    event = lax.axis_index("event")
    tile_at = lax.axis_index("tile")
    z = tile_at // plane
    depth = slots // plane
    group = events * plane
    me = event * plane + tile_at % plane

    def near_id(p):
        return (p // plane, z * plane + p % plane)

    def far_id(p):
        return (event, p * plane + tile_at % plane)

    send_s = (send0_s, send1_s, send2_s, send3_s)
    got_s = (got0_s, got1_s, got2_s, got3_s)
    barrier = pltpu.get_barrier_semaphore()

    def greet(to):
        pl.semaphore_signal(barrier, inc=1, device_id=to, device_id_type=MESH)

    def greet_tile(k, carry):
        greet((event, (tile_at + k) % slots))
        return carry

    def greet_event(k, carry):
        other = (event + 1 + k // plane) % events
        greet((other, z * plane + k % plane))
        return carry

    def swap_copy(index, to):
        return pltpu.make_async_remote_copy(
            src_ref=send_s[index].at[to],
            dst_ref=got_s[index].at[tile_at],
            send_sem=swap_send.at[index],
            recv_sem=swap_recv.at[index],
            device_id=(event, to),
            device_id_type=MESH,
        )

    def swap_start(index):
        def one(k, carry):
            swap_copy(index, (tile_at + k) % slots).start()
            return carry

        lax.fori_loop(1, slots, one, 0)
        got_s[index][tile_at] = send_s[index][tile_at]

    def swap_all(index):
        some = pl.ds(0, slots - 1)
        return pltpu.make_async_remote_copy(
            src_ref=send_s[index].at[some],
            dst_ref=got_s[index].at[some],
            send_sem=swap_send.at[index],
            recv_sem=swap_recv.at[index],
            device_id=(event, (tile_at + 1) % slots),
            device_id_type=MESH,
        )

    lax.fori_loop(1, slots, greet_tile, 0)
    lax.fori_loop(0, group - plane, greet_event, 0)
    fill_select(select_s)
    spread_weight(down_ref, down_s)

    def down_step(step, carry):
        tiles = fine_ref[rows_at(step, CHUNK)].reshape(CHUNK * 32, 256)
        x_taps = taps_to_lanes(mm_nt(select_s[...], tiles).astype(BF16))
        x_s[rows_at(step, step_rows // 4), :] = x_taps
        pre = to_rows(mm(x_taps, down_s[...]))
        at = rows_at(step, step_rows)
        pre_s[at, :] = pre
        act = (pre * sigmoid(pre)).astype(BF16)
        act_s[at, :] = act
        value_s[at, :] = act.astype(F32)
        read_edges(value_s, low_ref, right_ref, cell_ref, edges_s, step)
        return carry

    lax.fori_loop(0, steps, down_step, 0)
    fill_holder_routes(owner_ref, hold_s, slots)
    send_edges(hold_s, edges_s, send0_s)
    pl.semaphore_wait(barrier, slots - 1 + group - plane)
    swap_start(0)

    spread_weight(up_ref, up_s)
    for sy in range(3):
        for sx in range(3):
            weight = mid_ref[3 * sy + sx]
            conv_s[sx * 128 : (sx + 1) * 128, sy * 128 : (sy + 1) * 128] = weight
            back_s[sy * 128 : (sy + 1) * 128, sx * 128 : (sx + 1) * 128] = weight
    mid_acc[...] = jnp.zeros_like(mid_acc)
    up_acc[...] = jnp.zeros_like(up_acc)
    down_acc[...] = jnp.zeros_like(down_acc)

    def local_step(step, carry):
        tiles = cot_ref[rows_at(step, CHUNK)].reshape(CHUNK * 32, 256)
        g_taps = mm_nt(select_s[...], tiles)
        g_taps = g_taps * shown_ref[:, rows_at(step, CHUNK * 32)]
        g_taps = taps_to_lanes(g_taps.astype(BF16))
        g_s[rows_at(step, step_rows // 4), :] = g_taps
        at = rows_at(step, step_rows)
        grad_out_s[at, :] = to_rows(mm(g_taps, up_s[...])).astype(BF16)
        parts = mm(side_steps(value_s[at, :], False), conv_s[...])
        mid_s[at, :] = (
            row_step(parts[:, :128], -1) + parts[:, 128:256] + row_step(parts[:, 256:], 1)
        )
        return carry

    lax.fori_loop(0, steps, local_step, 0)
    swap_all(0).wait_recv()

    fill_routes(got0_s, route_s)
    gather_edges(route_s, got0_s, edge_s)
    cross_mid(mid_ref, edge_s, act_edge_s, reply_s)
    scatter_edges(route_s, reply_s, send1_s)
    swap_start(1)
    swap_all(1).wait_recv()

    def slope_step(step, carry):
        at = rows_at(step, step_rows)
        mid = mid_s[at, :] + foreign(low_ref, right_ref, reply_in_s, step)
        gate = sigmoid(mid)
        out_s[at, :] = (act_s[at, :].astype(F32) + mid * gate).astype(BF16)
        grad = grad_out_s[at, :].astype(F32) * (gate * (1.0 + mid * (1.0 - gate)))
        value_s[at, :] = grad.astype(BF16).astype(F32)
        read_edges(value_s, low_ref, right_ref, None, edges_s, step)
        return carry

    take_reply(hold_s, got1_s, reply_in_s)
    lax.fori_loop(0, steps, slope_step, 0)
    send_edges(hold_s, edges_s, send2_s)
    swap_start(2)

    def grad_step(step, carry):
        at = rows_at(step, step_rows)
        up_acc[...] += mm_tn(g_s[rows_at(step, step_rows // 4), :], to_lanes(out_s[at, :]))
        steps_of = side_steps(value_s[at, :], True)
        parts = mm_nt(steps_of, back_s[...])
        mid_s[at, :] = (
            grad_out_s[at, :].astype(F32)
            + row_step(parts[:, :128], 1)
            + parts[:, 128:256]
            + row_step(parts[:, 256:], -1)
        )
        act = act_s[at, :].astype(F32)
        acts = jnp.concatenate([row_step(act, s - 1).astype(BF16) for s in range(3)], axis=1)
        mid_acc[...] += mm_tn(acts, steps_of)
        return carry

    lax.fori_loop(0, steps, grad_step, 0)
    swap_all(2).wait_recv()

    gather_edges(route_s, got2_s, edge_s)
    cross_grad(mid_ref, edge_s, act_edge_s, reply_s, mid_acc)
    scatter_edges(route_s, reply_s, send3_s)
    swap_start(3)

    share = mine_s.shape[0] // group
    piece = share // pieces
    for tap in range(9):
        mine_s[tap * 128 : (tap + 1) * 128, :] = (
            mid_acc[
                tap // 3 * 128 : tap // 3 * 128 + 128, tap % 3 * 128 : tap % 3 * 128 + 128
            ]
            * scale
        ).astype(BF16)
    mine_s[1152:1280, :] = (fold_taps(up_acc) * scale).astype(BF16)
    if mine_s.shape[0] > 1280:
        mine_s[1280:, :] = jnp.zeros((mine_s.shape[0] - 1280, 128), BF16)

    def share_at(p):
        return pl.ds(pl.multiple_of(p * share, 16), share)

    def near_copy(to, slot):
        return pltpu.make_async_remote_copy(
            src_ref=mine_s.at[share_at(to)],
            dst_ref=near_s.at[slot],
            send_sem=near_send.at[to],
            recv_sem=near_recv.at[slot],
            device_id=near_id(to),
            device_id_type=MESH,
        )

    def far_copy(to, slot):
        return pltpu.make_async_remote_copy(
            src_ref=sum_s.at[to],
            dst_ref=far_s.at[slot],
            send_sem=far_send.at[to],
            recv_sem=far_recv.at[slot],
            device_id=far_id(to),
            device_id_type=MESH,
        )

    def fin_copy(to, slot):
        return pltpu.make_async_remote_copy(
            src_ref=fin_s.at[slot],
            dst_ref=fin_s.at[slot],
            send_sem=fin_send.at[to],
            recv_sem=fin_recv.at[slot],
            device_id=far_id(to),
            device_id_type=MESH,
        )

    def all_copy(to, slot):
        return pltpu.make_async_remote_copy(
            src_ref=low_s,
            dst_ref=all_s.at[share_at(slot)],
            send_sem=all_send.at[to],
            recv_sem=all_recv.at[slot],
            device_id=near_id(to),
            device_id_type=MESH,
        )

    def each(first, last, body):
        def one(k, carry):
            body(k)
            return carry

        lax.fori_loop(first, last, one, 0)

    each(1, group, lambda k: near_copy((me + k) % group, me).start())

    def take_near(k, total):
        p = (me + k) % group
        near_copy(p, p).wait_recv()
        return total + near_s[p].astype(F32)

    total = lax.fori_loop(1, group, take_near, mine_s[share_at(me), :].astype(F32))
    sum_s[...] = total.reshape(pieces, piece, 128)
    for to in range(pieces):

        @pl.when(z != to)
        def _():
            far_copy(to, z).start()

    @pl.when(z < pieces)
    def _():
        def take_far(k, total):
            p = (z + k) % depth
            far_copy(z, p).wait_recv()
            return total + far_s[p]

        fin_s[z] = lax.fori_loop(1, depth, take_far, sum_s[z])
        each(1, depth, lambda k: fin_copy((z + k) % depth, z).start())

    for p in range(pieces):

        @pl.when(z != p)
        def _():
            fin_copy(p, p).wait_recv()

    low_s[...] = fin_s[...].reshape(share, 128).astype(BF16)
    each(1, group, lambda k: all_copy((me + k) % group, me).start())
    all_s[share_at(me), :] = low_s[...]

    swap_all(3).wait_recv()

    def pre_step(step, carry):
        at = rows_at(step, step_rows)
        grad_act = mid_s[at, :] + foreign(low_ref, right_ref, reply_in_s, step)
        grad_act = grad_act.astype(BF16).astype(F32)
        grad_pre = to_lanes((grad_act * slope(pre_s[at, :])).astype(BF16))
        lanes_at = rows_at(step, step_rows // 4)
        down_acc[...] += mm_tn(x_s[lanes_at, :], grad_pre)
        g_s[lanes_at, :] = grad_pre
        return carry

    take_reply(hold_s, got3_s, reply_in_s)
    lax.fori_loop(0, steps, pre_step, 0)
    parts = mine2_s.shape[0]
    stride = group // parts
    my_part = me // stride
    reducer = me % stride == 0
    mine2_s[...] = (fold_taps(down_acc) * scale).astype(BF16).reshape(mine2_s.shape)

    def near2_copy(part, slot):
        return pltpu.make_async_remote_copy(
            src_ref=mine2_s.at[part],
            dst_ref=near2_s.at[slot],
            send_sem=near2_send.at[part],
            recv_sem=near2_recv.at[slot],
            device_id=near_id(part * stride),
            device_id_type=MESH,
        )

    def far2_copy(to, slot):
        return pltpu.make_async_remote_copy(
            src_ref=low2_s,
            dst_ref=far2_s.at[slot],
            send_sem=far2_send.at[to],
            recv_sem=far2_recv.at[slot],
            device_id=far_id(to),
            device_id_type=MESH,
        )

    def all2_copy(to, part):
        return pltpu.make_async_remote_copy(
            src_ref=fin2_s,
            dst_ref=all2_s.at[part],
            send_sem=all2_send.at[to],
            recv_sem=all2_recv.at[part],
            device_id=near_id(to),
            device_id_type=MESH,
        )

    for part in range(parts):

        @pl.when(me != part * stride)
        def _():
            near2_copy(part, me).start()

    def fine_step(step, carry):
        back = lanes_to_taps(mm_nt(g_s[rows_at(step, step_rows // 4), :], down_s[...]))
        high = back.astype(BF16)
        rest = (back - high.astype(F32)).astype(BF16)
        select = select_s[...]
        total = mm_tn(high, select) + mm_tn(rest, select)
        total += cot_ref[rows_at(step, CHUNK)].reshape(CHUNK * 32, 256).astype(F32)
        shown = [
            jnp.broadcast_to(active_ref[pl.ds(step * CHUNK + index, 1), :], (32, 128))
            for index in range(CHUNK)
        ]
        shown = jnp.concatenate(shown, axis=0)
        total = total * jnp.concatenate([shown, shown], axis=1)
        grad_fine_ref[rows_at(step, CHUNK)] = total.astype(BF16).reshape(CHUNK, 32, 256)
        return carry

    first, second = steps * 2 // 5, steps * 4 // 5
    lax.fori_loop(0, first, fine_step, 0)

    @pl.when(reducer)
    def _():
        def take(k, total):
            p = (me + k) % group
            near2_copy(my_part, p).wait_recv()
            return total + near2_s[p].astype(F32)

        low2_s[...] = lax.fori_loop(1, group, take, mine2_s[my_part].astype(F32)).astype(BF16)
        each(1, depth, lambda k: far2_copy((z + k) % depth, z).start())
        far2_s[z] = low2_s[...]

    lax.fori_loop(first, second, fine_step, 0)

    @pl.when(reducer)
    def _():
        def take(k):
            p = (z + k) % depth
            far2_copy(p, p).wait_recv()

        each(1, depth, take)
        fin2_s[...] = jnp.sum(far2_s[...].astype(F32), axis=0).astype(BF16)
        each(1, group, lambda k: all2_copy((me + k) % group, my_part).start())
        all2_s[my_part] = fin2_s[...]

    lax.fori_loop(second, steps, fine_step, 0)

    def take_all(k):
        p = (me + k) % group
        all_copy(p, p).wait_recv()

    each(1, group, take_all)
    grad_mid_ref[...] = all_s[:1152, :].astype(F32)
    grad_up_ref[...] = all_s[1152:1280, :].astype(F32)

    for index in range(4):
        swap_all(index).wait_send()

    def sent_near(k):
        p = (me + k) % group
        near_copy(p, me).wait_send()
        all_copy(p, me).wait_send()

    each(1, group, sent_near)
    for to in range(pieces):

        @pl.when(z != to)
        def _():
            far_copy(to, z).wait_send()

    @pl.when(z < pieces)
    def _():
        each(1, depth, lambda k: fin_copy((z + k) % depth, z).wait_send())

    for part in range(parts):

        @pl.when(me != part * stride)
        def _():
            near2_copy(part, me).wait_send()
            all2_copy(me, part).wait_recv()

    grad_down_ref[...] = all2_s[...].reshape(grad_down_ref.shape).astype(F32)

    @pl.when(reducer)
    def _():
        each(1, depth, lambda k: far2_copy((z + k) % depth, z).wait_send())
        each(1, group, lambda k: all2_copy((me + k) % group, my_part).wait_send())


def like(shape, dtype):
    return jax.ShapeDtypeStruct(shape, dtype)


def shards(plane, fine, cotangent, counts, parent, quadrant, down_weight, mid_weight, up_weight):
    number = fine.shape[1]
    slots = lax.axis_size("tile")
    events = lax.axis_size("event")
    coarse_dev = number // 4
    rows = number * PIXELS
    scale = 1.0 / math.sqrt(events * slots * number * 64)

    active = jnp.arange(number, dtype=jnp.int32) < counts[0, 0]
    shown = active.astype(F32)
    owner = jnp.where(active, parent[0] // coarse_dev, -1).astype(F32)
    cell = (parent[0] % coarse_dev * 4 + quadrant[0] + 1).astype(F32)
    low, right = (quadrant[0] // 2).astype(F32), (quadrant[0] % 2).astype(F32)

    def along(values, size):
        return jnp.broadcast_to(values[:, None], (number, size)).reshape(1, number * size)

    def across(values):
        return jnp.broadcast_to(values[:, None], (number, 128))

    places = (
        along(owner, EDGE_ROWS), along(shown, 32),
        across(low), across(right), across(cell), across(shown),
    )

    group = events * plane
    depth = slots // plane
    share = -(-1280 // (group * 16)) * 16
    pieces = max(n for n in range(1, share // 8 + 1) if share // 8 % n == 0 and n <= depth)
    piece = share // pieces
    dma = pltpu.SemaphoreType.DMA
    vm = pltpu.VMEM
    vmem = pl.BlockSpec(memory_space=vm)
    grad_fine, grad_down, grad_mid, grad_up = pl.pallas_call(
        functools.partial(block, events, plane, slots, pieces, scale),
        in_specs=[vmem] * 11,
        out_specs=[vmem] * 4,
        out_shape=[
            like((number, 32, 256), BF16),
            like((128, 128), F32),
            like((1152, 128), F32),
            like((128, 128), F32),
        ],
        scratch_shapes=[
            vm((256, 256), BF16),
            vm((512, 512), BF16),
            vm((512, 512), BF16),
            vm((384, 384), BF16),
            vm((384, 384), BF16),
            vm((slots * EDGE_ROWS, number * EDGE_ROWS), BF16),
            vm((number * EDGE_ROWS, 128), BF16),
            vm((number * EDGE_ROWS, 128), F32),
            vm((rows // 4, 512), BF16),
            vm((rows // 4, 512), BF16),
            vm((rows, 128), F32),
            vm((rows, 128), BF16),
            vm((rows, 128), F32),
            vm((rows, 128), F32),
            vm((rows, 128), BF16),
            vm((rows, 128), BF16),
            *[vm((slots, EDGE_ROWS, 128), BF16) for _ in range(8)],
            vm((slots * EDGE_ROWS, number * EDGE_ROWS), BF16),
            vm((2, 4, number * 2, 128), F32),
            vm((2, 4, number * 2, 128), BF16),
            vm((2, 4, number * 2, 128), F32),
            vm((384, 384), F32),
            vm((512, 512), F32),
            vm((512, 512), F32),
            vm((group * share, 128), BF16),
            vm((group, share, 128), BF16),
            vm((pieces, piece, 128), F32),
            vm((depth, piece, 128), F32),
            vm((pieces, piece, 128), F32),
            vm((share, 128), BF16),
            vm((group * share, 128), BF16),
            vm((8, 16, 128), BF16),
            vm((group, 16, 128), BF16),
            vm((16, 128), BF16),
            vm((depth, 16, 128), BF16),
            vm((16, 128), BF16),
            vm((8, 16, 128), BF16),
            dma((4,)),
            dma((4,)),
            dma((group,)),
            dma((group,)),
            dma((pieces,)),
            dma((depth,)),
            dma((depth,)),
            dma((pieces,)),
            dma((group,)),
            dma((group,)),
            dma((8,)),
            dma((group,)),
            dma((depth,)),
            dma((depth,)),
            dma((group,)),
            dma((8,)),
        ],
        compiler_params=pltpu.CompilerParams(
            collective_id=0, has_side_effects=True, vmem_limit_bytes=VMEM_LIMIT
        ),
        name="residual_block",
    )(*places, fine[0], cotangent[0], down_weight, mid_weight, up_weight)
    return (
        grad_fine[None],
        grad_down.reshape(4, 32, 128),
        grad_mid.reshape(9, 128, 128),
        grad_up.reshape(4, 32, 128),
    )


def solution(mesh):
    placed = (
        P("event", "tile", None, None),
        P("event", "tile", None, None),
        P("event", "tile"),
        P("event", "tile"),
        P("event", "tile"),
        P(),
        P(),
        P(),
    )
    return jax.shard_map(
        functools.partial(shards, 8),
        mesh=mesh,
        in_specs=placed,
        out_specs=(P("event", "tile", None, None), P(), P(), P()),
        check_vma=False,
    )
```

```python
import functools
import math

import jax
import jax.numpy as jnp
from jax import lax
from jax.experimental import pallas as pl
from jax.experimental.pallas import tpu as pltpu
from jax.sharding import PartitionSpec as P

MESH = pl.DeviceIdType.MESH
F32 = jnp.float32
BF16 = jnp.bfloat16
CHUNK = 16
PIXELS = 64
EDGE_ROWS = 16
VMEM_LIMIT = 60 * 1024 * 1024


def mm(a, b):
    return jnp.dot(a, b, preferred_element_type=F32)


def mm_nt(a, b):
    return lax.dot_general(a, b, (((1,), (1,)), ((), ())), preferred_element_type=F32)


def mm_tn(a, b):
    return lax.dot_general(a, b, (((0,), (0,)), ((), ())), preferred_element_type=F32)


def sigmoid(v):
    return 0.5 * jnp.tanh(0.5 * v) + 0.5


def slope(v):
    g = sigmoid(v)
    return g * (1.0 + v * (1.0 - g))


def shift8(x, step, fill=None):
    if step == 0:
        return x
    place = lax.broadcasted_iota(jnp.int32, x.shape, 1)
    moved = pltpu.roll(x, 7 if step > 0 else 1, 1)
    outside = place == (7 if step > 0 else 0)
    if fill is None:
        return jnp.where(outside, 0.0, moved)
    return jnp.where(outside, pltpu.roll(fill, 7 if step > 0 else 1, 1), moved)


def side_steps(x, flip):
    blocks = x.reshape(x.shape[0] // 8, 8, 128)
    parts = [shift8(blocks, 1 - s if flip else s - 1) for s in range(3)]
    return jnp.concatenate([part.reshape(x.shape).astype(BF16) for part in parts], axis=1)


def row_step(x, step):
    if step == 0:
        return x
    blocks = x.reshape(x.shape[0] // PIXELS, 8, 8, 128)
    zero = jnp.zeros((blocks.shape[0], 1, 8, 128), x.dtype)
    if step > 0:
        moved = jnp.concatenate([blocks[:, 1:], zero], axis=1)
    else:
        moved = jnp.concatenate([zero, blocks[:, :7]], axis=1)
    return moved.reshape(x.shape)


def spread_weight(weight_ref, spread_ref):
    spread_ref[...] = jnp.zeros_like(spread_ref)
    for tap in range(4):
        for tile in range(4):
            row = tap * 128 + tile * 32
            spread_ref[row : row + 32, tile * 128 : (tile + 1) * 128] = weight_ref[tap]


def to_lanes(x):
    groups = x.shape[0] // (4 * PIXELS)
    rows = []
    for group in range(groups):
        parts = [
            x[(group * 4 + tile) * PIXELS : (group * 4 + tile + 1) * PIXELS] for tile in range(4)
        ]
        rows.append(jnp.concatenate(parts, axis=1))
    return jnp.concatenate(rows, axis=0)


def to_rows(x):
    groups = x.shape[0] // PIXELS
    parts = []
    for group in range(groups):
        for tile in range(4):
            parts.append(x[group * PIXELS : (group + 1) * PIXELS, tile * 128 : (tile + 1) * 128])
    return jnp.concatenate(parts, axis=0)


def taps_to_lanes(x):
    groups = x.shape[1] // 128
    rows = []
    for group in range(groups):
        parts = [
            x[tap * PIXELS : (tap + 1) * PIXELS, group * 128 : (group + 1) * 128]
            for tap in range(4)
        ]
        rows.append(jnp.concatenate(parts, axis=1))
    return jnp.concatenate(rows, axis=0)


def lanes_to_taps(x):
    groups = x.shape[0] // PIXELS
    columns = []
    for group in range(groups):
        parts = [
            x[group * PIXELS : (group + 1) * PIXELS, tap * 128 : (tap + 1) * 128]
            for tap in range(4)
        ]
        columns.append(jnp.concatenate(parts, axis=0))
    return jnp.concatenate(columns, axis=1)


def fill_select(select_s):
    row = lax.broadcasted_iota(jnp.int32, (256, 256), 0)
    column = lax.broadcasted_iota(jnp.int32, (256, 256), 1)
    tap, i, j = row // 64, row // 8 % 8, row % 8
    meet = column == 16 * (2 * i + tap // 2) + 2 * j + tap % 2
    select_s[...] = jnp.where(meet, 1.0, 0.0).astype(BF16)


def place_of(quad):
    return (1 - quad // 2) * 7, (1 - quad % 2) * 7


def corner(x, at):
    return jnp.broadcast_to(x[:, at : at + 1, :], x.shape)


def pack(parts):
    rows = parts[0].shape[0] * 8
    return jnp.concatenate([part.reshape(rows, 128).astype(BF16) for part in parts], axis=1)


def edges_of(edge_s, number):
    rows, cols = [], []
    for quad in range(4):
        at_y, at_x = place_of(quad)
        row = edge_s[0, quad, : number * 8, :].reshape(number, 8, 128)
        col = edge_s[1, quad, : number * 8, :].reshape(number, 8, 128)
        place = lax.broadcasted_iota(jnp.int32, row.shape, 1)
        rows.append(row)
        cols.append(jnp.where(place == at_y, corner(row, at_x), col))
    return rows, cols


def write_reply(reply_s, quad, row, col):
    at_y, at_x = place_of(quad)
    rows = row.shape[0] * 8
    place = lax.broadcasted_iota(jnp.int32, row.shape, 1)
    row = row + jnp.where(place == at_x, corner(col, at_y), 0.0)
    reply_s[0, quad, :rows, :] = row.reshape(rows, 128)
    reply_s[1, quad, :rows, :] = jnp.where(place == at_y, 0.0, col).reshape(rows, 128)


def fold_taps(acc):
    taps = []
    for tap in range(4):
        part = jnp.zeros((32, 128), F32)
        for tile in range(4):
            row = tap * 128 + tile * 32
            part += acc[row : row + 32, tile * 128 : (tile + 1) * 128]
        taps.append(part)
    return jnp.concatenate(taps, axis=0)


def rows_at(step, size):
    return pl.ds(pl.multiple_of(step * size, size), size)


def side_of(ref, tile):
    return jnp.broadcast_to(ref[pl.ds(tile, 1), :], (8, 128))


def read_edges(value_s, low_ref, right_ref, cell_ref, edges_s, step):
    place = lax.broadcasted_iota(jnp.int32, (8, 128), 0)
    for index in range(CHUNK):
        tile = step * CHUNK + index
        start = pl.multiple_of(tile * PIXELS, PIXELS)
        low, right = side_of(low_ref, tile), side_of(right_ref, tile)
        top = value_s[pl.ds(start, 8), :]
        bottom = value_s[pl.ds(start + 56, 8), :]
        left = value_s[pl.ds(start, 8, stride=8), :]
        end = value_s[pl.ds(start + 7, 8, stride=8), :]
        row = bottom * (1.0 - low) + top * low
        col = end * (1.0 - right) + left * right
        col = col * (1.0 - low) + pltpu.roll(col, 7, 0) * low
        if cell_ref is not None:
            col = jnp.where(place == 7, side_of(cell_ref, tile), col)
        at = pl.ds(pl.multiple_of(tile * EDGE_ROWS, EDGE_ROWS), EDGE_ROWS)
        edges_s[at, :] = jnp.concatenate([row, col], axis=0).astype(BF16)


def fill_holder_routes(owner_ref, hold_s, slots):
    columns = hold_s.shape[1]
    column = lax.broadcasted_iota(jnp.int32, (EDGE_ROWS, columns), 1)
    row = lax.broadcasted_iota(jnp.int32, (EDGE_ROWS, columns), 0)
    here = jnp.where(row == column % EDGE_ROWS, 1.0, 0.0)
    owner = jnp.broadcast_to(owner_ref[0:1, :], (EDGE_ROWS, columns))

    def one(slot, carry):
        at = pl.ds(pl.multiple_of(slot * EDGE_ROWS, EDGE_ROWS), EDGE_ROWS)
        hold_s[at, :] = jnp.where(owner == slot.astype(F32), here, 0.0).astype(BF16)
        return carry

    lax.fori_loop(0, slots, one, 0, unroll=2)


def fill_routes(got_ref, route_s):
    slots, columns = got_ref.shape[0], route_s.shape[1]
    column = lax.broadcasted_iota(jnp.int32, (EDGE_ROWS, columns), 1)
    row = lax.broadcasted_iota(jnp.int32, (EDGE_ROWS, columns), 0)
    kind, rest = column // (columns // 2), column % (columns // 2)
    quad, rest = rest // (columns // 8), rest % (columns // 8)
    tile, place = rest // 8, rest % 8
    turned = jnp.where((kind == 1) & (quad >= 2), (place + 7) % 8, place)
    here = jnp.where(row == kind * 8 + turned, 1.0, 0.0)
    cell = (tile * 4 + quad + 1).astype(F32)

    def one(slot, carry):
        tag = got_ref[slot].astype(F32)[EDGE_ROWS - 1 :]
        tag = jnp.concatenate([jnp.broadcast_to(tag, (EDGE_ROWS, 128))] * (columns // 128), axis=1)
        at = pl.ds(pl.multiple_of(slot * EDGE_ROWS, EDGE_ROWS), EDGE_ROWS)
        route_s[at, :] = jnp.where(tag == cell, here, 0.0).astype(BF16)
        return carry

    lax.fori_loop(0, slots, one, 0, unroll=2)


def gather_edges(route_s, got_ref, edge_s):
    rows = got_ref.shape[0] * EDGE_ROWS
    turned = mm_tn(got_ref[...].reshape(rows, 128), route_s[...])
    edge_s[...] = turned.T.reshape(edge_s.shape)


def scatter_edges(route_s, reply_s, send_ref):
    flat = reply_s[...].reshape(route_s.shape[1], 128).astype(BF16)
    send_ref[...] = mm(route_s[...], flat).astype(BF16).reshape(send_ref.shape)


def send_edges(hold_s, edges_s, send_ref):
    send_ref[...] = mm(hold_s[...], edges_s[...]).astype(BF16).reshape(send_ref.shape)


def take_reply(hold_s, got_ref, reply_in_s):
    rows = got_ref.shape[0] * EDGE_ROWS
    reply_in_s[...] = mm_tn(got_ref[...].reshape(rows, 128), hold_s[...]).T


def cross_mid(mid_ref, edge_s, act_edge_s, reply_s):
    number = edge_s.shape[2] // 8
    act_row, act_col = edges_of(edge_s, number)
    for quad in range(4):
        low, right = quad // 2, quad % 2
        act_edge_s[0, quad] = act_row[quad].reshape(number * 8, 128).astype(BF16)
        act_edge_s[1, quad] = act_col[quad].reshape(number * 8, 128).astype(BF16)
        across, beyond, beside = act_row[quad ^ 2], act_row[quad ^ 3], act_col[quad ^ 1]
        fills = [beyond if right == 1 else None, None, beyond if right == 0 else None]
        sy, sx = 2 - 2 * low, 2 - 2 * right
        patch = pack([shift8(across, s - 1, fills[s]) for s in range(3)])
        weight = jnp.concatenate([mid_ref[3 * sy + s] for s in range(3)], axis=0)
        row = mm(patch, weight).reshape(number, 8, 128)
        patch = pack([shift8(beside, s - 1) for s in range(3)])
        weight = jnp.concatenate([mid_ref[3 * s + sx] for s in range(3)], axis=0)
        col = mm(patch, weight).reshape(number, 8, 128)
        write_reply(reply_s, quad, row, col)


def cross_grad(mid_ref, edge_s, act_edge_s, reply_s, cross_ref):
    number = edge_s.shape[2] // 8
    grad_row, grad_col = edges_of(edge_s, number)
    for quad in range(4):
        low, right = quad // 2, quad % 2
        across, beyond, beside = grad_row[quad ^ 2], grad_row[quad ^ 3], grad_col[quad ^ 1]
        fills = [beyond if right == 0 else None, None, beyond if right == 1 else None]
        sy, sx = 2 * low, 2 * right
        patch = pack([shift8(across, 1 - s, fills[s]) for s in range(3)])
        weight = jnp.concatenate([mid_ref[3 * sy + s] for s in range(3)], axis=1)
        row = mm_nt(patch, weight).reshape(number, 8, 128)
        cross_ref[sy * 128 : (sy + 1) * 128, :] += mm_tn(act_edge_s[0, quad], patch)
        patch = pack([shift8(beside, 1 - s) for s in range(3)])
        weight = jnp.concatenate([mid_ref[3 * s + sx] for s in range(3)], axis=1)
        col = mm_nt(patch, weight).reshape(number, 8, 128)
        part = mm_tn(act_edge_s[1, quad], patch)
        for s in range(3):
            cross_ref[s * 128 : (s + 1) * 128, sx * 128 : (sx + 1) * 128] += (
                part[:, s * 128 : (s + 1) * 128]
            )
        write_reply(reply_s, quad, row, col)


def foreign(low_ref, right_ref, reply_in_s, step):
    place = lax.broadcasted_iota(jnp.int32, (8, 128), 0)
    parts = []
    for index in range(CHUNK):
        tile = step * CHUNK + index
        start = pl.multiple_of(tile * EDGE_ROWS, EDGE_ROWS)
        low, right = side_of(low_ref, tile), side_of(right_ref, tile)
        row = reply_in_s[pl.ds(start, 8), :]
        col = reply_in_s[pl.ds(start + 8, 8), :]
        col = col * (1.0 - low) + pltpu.roll(col, 1, 0) * low
        mask = jnp.where(place == 0, right, jnp.where(place == 7, 1.0 - right, 0.0))
        for i in range(8):
            part = mask * jnp.broadcast_to(col[i : i + 1], (8, 128))
            if i == 0:
                part += row * low
            elif i == 7:
                part += row * (1.0 - low)
            parts.append(part)
    return jnp.concatenate(parts, axis=0)


def spread_places(place_ref, owner_s, shown_s, across):
    places = place_ref[...].astype(BF16)
    lanes = places.shape[1]
    for target, size in ((owner_s, EDGE_ROWS), (shown_s, 32)):
        row = lax.broadcasted_iota(jnp.int32, (lanes, target.shape[1]), 0)
        column = lax.broadcasted_iota(jnp.int32, (lanes, target.shape[1]), 1)
        target[...] = mm(places, jnp.where(column // size == row, 1.0, 0.0).astype(BF16))
    place = lax.broadcasted_iota(jnp.int32, (16, 128), 0)
    for index, target in enumerate(across):
        target[...] = mm_tn(places, jnp.where(place == index + 1, 1.0, 0.0).astype(BF16))


def block(
    events, plane, slots, pieces, scale,
    place_ref, fine_hbm, cot_hbm, down_hbm, mid_hbm, up_hbm,
    grad_fine_ref, grad_down_ref, grad_mid_ref, grad_up_ref,
    select_s, down_s, up_s, fine_ref, cot_ref, down_ref, mid_ref, up_ref,
    conv_s, back_s, owner_s, shown_s, low_s, right_s, cell_s, active_s, hold_s, edges_s, reply_in_s,
    x_s, g_s, pre_s, act_s, value_s, mid_s, grad_out_s, out_s,
    send0_s, send1_s, send2_s, send3_s, got0_s, got1_s, got2_s, got3_s, route_s, edge_s, act_edge_s, reply_s,
    mid_acc, up_acc, down_acc,
    mine_s, near_s, sum_s, far_s, fin_s, half_s, all_s,
    mine2_s, near2_s, low2_s, far2_s, fin2_s, all2_s,
    load_sem, swap_send, swap_recv,
    near_send, near_recv, far_send, far_recv, fin_send, fin_recv, all_send, all_recv,
    near2_send, near2_recv, far2_send, far2_recv, all2_send, all2_recv,
):
    number = fine_ref.shape[0]
    steps = number // CHUNK
    step_rows = CHUNK * PIXELS
    event = lax.axis_index("event")
    tile_at = lax.axis_index("tile")
    z = tile_at // plane
    depth = slots // plane
    group = events * plane
    me = event * plane + tile_at % plane

    def near_id(p):
        return (p // plane, z * plane + p % plane)

    def far_id(p):
        return (event, p * plane + tile_at % plane)

    send_s = (send0_s, send1_s, send2_s, send3_s)
    got_s = (got0_s, got1_s, got2_s, got3_s)
    loads = [
        pltpu.make_async_copy(source, target, load_sem.at[index])
        for index, (source, target) in enumerate(
            (
                (fine_hbm, fine_ref),
                (down_hbm, down_ref),
                (cot_hbm, cot_ref),
                (up_hbm, up_ref),
                (mid_hbm, mid_ref),
            )
        )
    ]
    for load in loads:
        load.start()
    barrier = pltpu.get_barrier_semaphore()

    def greet(to):
        pl.semaphore_signal(barrier, inc=1, device_id=to, device_id_type=MESH)

    def greet_tile(k, carry):
        greet((event, (tile_at + k) % slots))
        return carry

    def greet_event(k, carry):
        other = (event + 1 + k // plane) % events
        greet((other, z * plane + k % plane))
        return carry

    def swap_copy(index, to):
        return pltpu.make_async_remote_copy(
            src_ref=send_s[index].at[to],
            dst_ref=got_s[index].at[tile_at],
            send_sem=swap_send.at[index],
            recv_sem=swap_recv.at[index],
            device_id=(event, to),
            device_id_type=MESH,
        )

    def swap_start(index):
        def one(k, carry):
            swap_copy(index, (tile_at + k) % slots).start()
            return carry

        lax.fori_loop(1, slots, one, 0)
        got_s[index][tile_at] = send_s[index][tile_at]

    def swap_all(index):
        some = pl.ds(0, slots - 1)
        return pltpu.make_async_remote_copy(
            src_ref=send_s[index].at[some],
            dst_ref=got_s[index].at[some],
            send_sem=swap_send.at[index],
            recv_sem=swap_recv.at[index],
            device_id=(event, (tile_at + 1) % slots),
            device_id_type=MESH,
        )

    per_tile, per_event = (slots - 1) // steps, (group - plane) // steps
    for k in range(1 + per_tile * steps, slots):
        greet_tile(k, 0)
    for k in range(per_event * steps, group - plane):
        greet_event(k, 0)
    spread_places(place_ref, owner_s, shown_s, (low_s, right_s, cell_s, active_s))
    fill_select(select_s)
    loads[0].wait()
    loads[1].wait()
    spread_weight(down_ref, down_s)

    def down_step(step, carry):
        for k in range(per_tile):
            greet_tile(1 + step * per_tile + k, 0)
        for k in range(per_event):
            greet_event(step * per_event + k, 0)
        tiles = fine_ref[rows_at(step, CHUNK)].reshape(CHUNK * 32, 256)
        x_taps = taps_to_lanes(mm_nt(select_s[...], tiles).astype(BF16))
        x_s[rows_at(step, step_rows // 4), :] = x_taps
        pre = to_rows(mm(x_taps, down_s[...]))
        at = rows_at(step, step_rows)
        pre_s[at, :] = pre
        act = (pre * sigmoid(pre)).astype(BF16)
        act_s[at, :] = act
        value_s[at, :] = act.astype(F32)
        read_edges(value_s, low_s, right_s, cell_s, edges_s, step)
        return carry

    lax.fori_loop(0, steps, down_step, 0)
    fill_holder_routes(owner_s, hold_s, slots)
    send_edges(hold_s, edges_s, send0_s)
    pl.semaphore_wait(barrier, slots - 1 + group - plane)
    swap_start(0)

    for load in loads[2:]:
        load.wait()
    spread_weight(up_ref, up_s)
    for sy in range(3):
        for sx in range(3):
            weight = mid_ref[3 * sy + sx]
            conv_s[sx * 128 : (sx + 1) * 128, sy * 128 : (sy + 1) * 128] = weight
            back_s[sy * 128 : (sy + 1) * 128, sx * 128 : (sx + 1) * 128] = weight
    mid_acc[...] = jnp.zeros_like(mid_acc)
    up_acc[...] = jnp.zeros_like(up_acc)
    down_acc[...] = jnp.zeros_like(down_acc)

    def local_step(step, carry):
        tiles = cot_ref[rows_at(step, CHUNK)].reshape(CHUNK * 32, 256)
        g_taps = mm_nt(select_s[...], tiles)
        g_taps = g_taps * shown_s[4:5, rows_at(step, CHUNK * 32)]
        g_taps = taps_to_lanes(g_taps.astype(BF16))
        g_s[rows_at(step, step_rows // 4), :] = g_taps
        at = rows_at(step, step_rows)
        grad_out_s[at, :] = to_rows(mm(g_taps, up_s[...])).astype(BF16)
        parts = mm(side_steps(value_s[at, :], False), conv_s[...])
        mid_s[at, :] = (
            row_step(parts[:, :128], -1) + parts[:, 128:256] + row_step(parts[:, 256:], 1)
        )
        return carry

    lax.fori_loop(0, steps, local_step, 0)
    swap_all(0).wait_recv()

    fill_routes(got0_s, route_s)
    gather_edges(route_s, got0_s, edge_s)
    cross_mid(mid_ref, edge_s, act_edge_s, reply_s)
    scatter_edges(route_s, reply_s, send1_s)
    swap_start(1)
    swap_all(1).wait_recv()

    def slope_step(step, carry):
        at = rows_at(step, step_rows)
        mid = mid_s[at, :] + foreign(low_s, right_s, reply_in_s, step)
        gate = sigmoid(mid)
        out_s[at, :] = (act_s[at, :].astype(F32) + mid * gate).astype(BF16)
        grad = grad_out_s[at, :].astype(F32) * (gate * (1.0 + mid * (1.0 - gate)))
        value_s[at, :] = grad.astype(BF16).astype(F32)
        read_edges(value_s, low_s, right_s, None, edges_s, step)
        return carry

    take_reply(hold_s, got1_s, reply_in_s)
    lax.fori_loop(0, steps, slope_step, 0)
    send_edges(hold_s, edges_s, send2_s)
    swap_start(2)

    def grad_step(step, carry):
        at = rows_at(step, step_rows)
        up_acc[...] += mm_tn(g_s[rows_at(step, step_rows // 4), :], to_lanes(out_s[at, :]))
        steps_of = side_steps(value_s[at, :], True)
        parts = mm_nt(steps_of, back_s[...])
        mid_s[at, :] = (
            grad_out_s[at, :].astype(F32)
            + row_step(parts[:, :128], 1)
            + parts[:, 128:256]
            + row_step(parts[:, 256:], -1)
        )
        act = act_s[at, :].astype(F32)
        acts = jnp.concatenate([row_step(act, s - 1).astype(BF16) for s in range(3)], axis=1)
        mid_acc[...] += mm_tn(acts, steps_of)
        return carry

    lax.fori_loop(0, steps, grad_step, 0)
    swap_all(2).wait_recv()

    gather_edges(route_s, got2_s, edge_s)
    cross_grad(mid_ref, edge_s, act_edge_s, reply_s, mid_acc)
    scatter_edges(route_s, reply_s, send3_s)
    swap_start(3)

    share = mine_s.shape[0] // group
    piece = share // pieces
    for tap in range(9):
        mine_s[tap * 128 : (tap + 1) * 128, :] = (
            mid_acc[
                tap // 3 * 128 : tap // 3 * 128 + 128, tap % 3 * 128 : tap % 3 * 128 + 128
            ]
            * scale
        ).astype(BF16)
    mine_s[1152:1280, :] = (fold_taps(up_acc) * scale).astype(BF16)
    if mine_s.shape[0] > 1280:
        mine_s[1280:, :] = jnp.zeros((mine_s.shape[0] - 1280, 128), BF16)

    def share_at(p):
        return pl.ds(pl.multiple_of(p * share, 16), share)

    def near_copy(to, slot):
        return pltpu.make_async_remote_copy(
            src_ref=mine_s.at[share_at(to)],
            dst_ref=near_s.at[slot],
            send_sem=near_send.at[to],
            recv_sem=near_recv.at[slot],
            device_id=near_id(to),
            device_id_type=MESH,
        )

    def far_copy(to, slot):
        return pltpu.make_async_remote_copy(
            src_ref=sum_s.at[to],
            dst_ref=far_s.at[slot],
            send_sem=far_send.at[to],
            recv_sem=far_recv.at[slot],
            device_id=far_id(to),
            device_id_type=MESH,
        )

    def fin_copy(to, slot):
        return pltpu.make_async_remote_copy(
            src_ref=fin_s.at[slot],
            dst_ref=fin_s.at[slot],
            send_sem=fin_send.at[to],
            recv_sem=fin_recv.at[slot],
            device_id=far_id(to),
            device_id_type=MESH,
        )

    def all_copy(to, slot):
        return pltpu.make_async_remote_copy(
            src_ref=half_s,
            dst_ref=all_s.at[share_at(slot)],
            send_sem=all_send.at[to],
            recv_sem=all_recv.at[slot],
            device_id=near_id(to),
            device_id_type=MESH,
        )

    def each(first, last, body):
        def one(k, carry):
            body(k)
            return carry

        lax.fori_loop(first, last, one, 0)

    each(1, group, lambda k: near_copy((me + k) % group, me).start())

    def take_near(k, total):
        p = (me + k) % group
        near_copy(p, p).wait_recv()
        return total + near_s[p].astype(F32)

    total = lax.fori_loop(1, group, take_near, mine_s[share_at(me), :].astype(F32))
    sum_s[...] = total.reshape(pieces, piece, 128)
    for to in range(pieces):

        @pl.when(z != to)
        def _():
            far_copy(to, z).start()

    @pl.when(z < pieces)
    def _():
        def take_far(k, total):
            p = (z + k) % depth
            far_copy(z, p).wait_recv()
            return total + far_s[p]

        fin_s[z] = lax.fori_loop(1, depth, take_far, sum_s[z])
        each(1, depth, lambda k: fin_copy((z + k) % depth, z).start())

    swap_all(3).wait_recv()

    def pre_step(step, carry):
        at = rows_at(step, step_rows)
        grad_act = mid_s[at, :] + foreign(low_s, right_s, reply_in_s, step)
        grad_act = grad_act.astype(BF16).astype(F32)
        grad_pre = to_lanes((grad_act * slope(pre_s[at, :])).astype(BF16))
        lanes_at = rows_at(step, step_rows // 4)
        down_acc[...] += mm_tn(x_s[lanes_at, :], grad_pre)
        g_s[lanes_at, :] = grad_pre
        return carry

    take_reply(hold_s, got3_s, reply_in_s)
    lax.fori_loop(0, steps, pre_step, 0)
    parts = mine2_s.shape[0]
    stride = group // parts
    my_part = me // stride
    reducer = me % stride == 0
    mine2_s[...] = (fold_taps(down_acc) * scale).astype(BF16).reshape(mine2_s.shape)

    def near2_copy(part, slot):
        return pltpu.make_async_remote_copy(
            src_ref=mine2_s.at[part],
            dst_ref=near2_s.at[slot],
            send_sem=near2_send.at[part],
            recv_sem=near2_recv.at[slot],
            device_id=near_id(part * stride),
            device_id_type=MESH,
        )

    def far2_copy(to, slot):
        return pltpu.make_async_remote_copy(
            src_ref=low2_s,
            dst_ref=far2_s.at[slot],
            send_sem=far2_send.at[to],
            recv_sem=far2_recv.at[slot],
            device_id=far_id(to),
            device_id_type=MESH,
        )

    def all2_copy(to, part):
        return pltpu.make_async_remote_copy(
            src_ref=fin2_s,
            dst_ref=all2_s.at[part],
            send_sem=all2_send.at[to],
            recv_sem=all2_recv.at[part],
            device_id=near_id(to),
            device_id_type=MESH,
        )

    for part in range(parts):

        @pl.when(me != part * stride)
        def _():
            near2_copy(part, me).start()

    for p in range(pieces):

        @pl.when(z != p)
        def _():
            fin_copy(p, p).wait_recv()

    half_s[...] = fin_s[...].reshape(share, 128).astype(BF16)
    each(1, group, lambda k: all_copy((me + k) % group, me).start())
    all_s[share_at(me), :] = half_s[...]

    def fine_step(step, carry):
        back = lanes_to_taps(mm_nt(g_s[rows_at(step, step_rows // 4), :], down_s[...]))
        high = back.astype(BF16)
        rest = (back - high.astype(F32)).astype(BF16)
        select = select_s[...]
        total = mm_tn(high, select) + mm_tn(rest, select)
        total += cot_ref[rows_at(step, CHUNK)].reshape(CHUNK * 32, 256).astype(F32)
        shown = [
            jnp.broadcast_to(active_s[pl.ds(step * CHUNK + index, 1), :], (32, 128))
            for index in range(CHUNK)
        ]
        shown = jnp.concatenate(shown, axis=0)
        total = total * jnp.concatenate([shown, shown], axis=1)
        grad_fine_ref[rows_at(step, CHUNK)] = total.astype(BF16).reshape(CHUNK, 32, 256)
        return carry

    first, second = steps * 2 // 5, steps * 4 // 5
    lax.fori_loop(0, first, fine_step, 0)

    @pl.when(reducer)
    def _():
        def take(k, total):
            p = (me + k) % group
            near2_copy(my_part, p).wait_recv()
            return total + near2_s[p].astype(F32)

        low2_s[...] = lax.fori_loop(1, group, take, mine2_s[my_part].astype(F32)).astype(BF16)
        each(1, depth, lambda k: far2_copy((z + k) % depth, z).start())
        far2_s[z] = low2_s[...]

    lax.fori_loop(first, second, fine_step, 0)

    @pl.when(reducer)
    def _():
        def take(k):
            p = (z + k) % depth
            far2_copy(p, p).wait_recv()

        each(1, depth, take)
        fin2_s[...] = jnp.sum(far2_s[...].astype(F32), axis=0).astype(BF16)
        each(1, group, lambda k: all2_copy((me + k) % group, my_part).start())
        all2_s[my_part] = fin2_s[...]

    lax.fori_loop(second, steps, fine_step, 0)

    def take_all(k):
        p = (me + k) % group
        all_copy(p, p).wait_recv()

    each(1, group, take_all)
    grad_mid_ref[...] = all_s[:1152, :].astype(F32)
    grad_up_ref[...] = all_s[1152:1280, :].astype(F32)

    for index in range(4):
        swap_all(index).wait_send()

    def sent_near(k):
        p = (me + k) % group
        near_copy(p, me).wait_send()
        all_copy(p, me).wait_send()

    each(1, group, sent_near)
    for to in range(pieces):

        @pl.when(z != to)
        def _():
            far_copy(to, z).wait_send()

    @pl.when(z < pieces)
    def _():
        each(1, depth, lambda k: fin_copy((z + k) % depth, z).wait_send())

    for part in range(parts):

        @pl.when(me != part * stride)
        def _():
            near2_copy(part, me).wait_send()
            all2_copy(me, part).wait_recv()

    grad_down_ref[...] = all2_s[...].reshape(grad_down_ref.shape).astype(F32)

    @pl.when(reducer)
    def _():
        each(1, depth, lambda k: far2_copy((z + k) % depth, z).wait_send())
        each(1, group, lambda k: all2_copy((me + k) % group, my_part).wait_send())


def like(shape, dtype):
    return jax.ShapeDtypeStruct(shape, dtype)


def shards(plane, fine, cotangent, counts, parent, quadrant, down_weight, mid_weight, up_weight):
    number = fine.shape[1]
    slots = lax.axis_size("tile")
    events = lax.axis_size("event")
    coarse_dev = number // 4
    rows = number * PIXELS
    scale = 1.0 / math.sqrt(events * slots * number * 64)

    active = jnp.arange(number, dtype=jnp.int32) < counts[0, 0]
    shown = active.astype(F32)
    owner = jnp.where(active, parent[0] // coarse_dev, -1).astype(F32)
    cell = (parent[0] % coarse_dev * 4 + quadrant[0] + 1).astype(F32)
    low, right = (quadrant[0] // 2).astype(F32), (quadrant[0] % 2).astype(F32)

    lanes = -(-number // 128) * 128
    places = jnp.stack([owner, low, right, cell, shown])
    places = jnp.pad(places, ((0, 11), (0, lanes - number)))

    group = events * plane
    depth = slots // plane
    share = -(-1280 // (group * 16)) * 16
    pieces = max(n for n in range(1, share // 8 + 1) if share // 8 % n == 0 and n <= depth)
    piece = share // pieces
    dma = pltpu.SemaphoreType.DMA
    vm = pltpu.VMEM
    vmem = pl.BlockSpec(memory_space=vm)
    grad_fine, grad_down, grad_mid, grad_up = pl.pallas_call(
        functools.partial(block, events, plane, slots, pieces, scale),
        in_specs=[vmem] + [pl.BlockSpec(memory_space=pltpu.HBM)] * 5,
        out_specs=[vmem] * 4,
        out_shape=[
            like((number, 32, 256), BF16),
            like((128, 128), F32),
            like((1152, 128), F32),
            like((128, 128), F32),
        ],
        scratch_shapes=[
            vm((256, 256), BF16),
            vm((512, 512), BF16),
            vm((512, 512), BF16),
            vm((number, 32, 256), BF16),
            vm((number, 32, 256), BF16),
            vm((4, 32, 128), BF16),
            vm((9, 128, 128), BF16),
            vm((4, 32, 128), BF16),
            vm((384, 384), BF16),
            vm((384, 384), BF16),
            vm((16, number * EDGE_ROWS), F32),
            vm((16, number * 32), F32),
            *[vm((lanes, 128), F32) for _ in range(4)],
            vm((slots * EDGE_ROWS, number * EDGE_ROWS), BF16),
            vm((number * EDGE_ROWS, 128), BF16),
            vm((number * EDGE_ROWS, 128), F32),
            vm((rows // 4, 512), BF16),
            vm((rows // 4, 512), BF16),
            vm((rows, 128), F32),
            vm((rows, 128), BF16),
            vm((rows + 8, 128), F32),
            vm((rows, 128), F32),
            vm((rows, 128), BF16),
            vm((rows, 128), BF16),
            *[vm((slots, EDGE_ROWS, 128), BF16) for _ in range(8)],
            vm((slots * EDGE_ROWS, number * EDGE_ROWS), BF16),
            vm((2, 4, number * 2, 128), F32),
            vm((2, 4, number * 2, 128), BF16),
            vm((2, 4, number * 2, 128), F32),
            vm((384, 384), F32),
            vm((512, 512), F32),
            vm((512, 512), F32),
            vm((group * share, 128), BF16),
            vm((group, share, 128), BF16),
            vm((pieces, piece, 128), F32),
            vm((depth, piece, 128), F32),
            vm((pieces, piece, 128), F32),
            vm((share, 128), BF16),
            vm((group * share, 128), BF16),
            vm((8, 16, 128), BF16),
            vm((group, 16, 128), BF16),
            vm((16, 128), BF16),
            vm((depth, 16, 128), BF16),
            vm((16, 128), BF16),
            vm((8, 16, 128), BF16),
            dma((5,)),
            dma((4,)),
            dma((4,)),
            dma((group,)),
            dma((group,)),
            dma((pieces,)),
            dma((depth,)),
            dma((depth,)),
            dma((pieces,)),
            dma((group,)),
            dma((group,)),
            dma((8,)),
            dma((group,)),
            dma((depth,)),
            dma((depth,)),
            dma((group,)),
            dma((8,)),
        ],
        compiler_params=pltpu.CompilerParams(
            collective_id=0, has_side_effects=True, vmem_limit_bytes=VMEM_LIMIT
        ),
        name="residual_block",
    )(places, fine[0], cotangent[0], down_weight, mid_weight, up_weight)
    return (
        grad_fine[None],
        grad_down.reshape(4, 32, 128),
        grad_mid.reshape(9, 128, 128),
        grad_up.reshape(4, 32, 128),
    )


def solution(mesh):
    placed = (
        P("event", "tile", None, None),
        P("event", "tile", None, None),
        P("event", "tile"),
        P("event", "tile"),
        P("event", "tile"),
        P(),
        P(),
        P(),
    )
    return jax.shard_map(
        functools.partial(shards, 8),
        mesh=mesh,
        in_specs=placed,
        out_specs=(P("event", "tile", None, None), P(), P(), P()),
        check_vma=False,
    )
```
